256 devices in a mesh: lat: 32 (over y, z), chan: 8 (over x, core).
Axes of the slice: x: 4, y: 4, z: 8, core: 2. Of those that a mesh axis runs over, the one named last changes fastest.
Arguments:
- grid_in: bfloat16 [768, 1440, 256], P('lat', None, 'chan'), may hold values from -6 to 6
- pairing: int32 [384], replicated, may hold values from -1 to 359, as said below
- offsets: int32 [33], replicated, may hold values from 0 to 384, as said below
- legendre: bfloat16 [384, 721, 384], P('lat'), may hold values from -0.3125 to 0.3125
- degree_mix: bfloat16 [720, 256, 256], P(None, 'lat', 'chan'), may hold values from -0.375 to 0.375
- w_in: bfloat16 [256, 512], replicated, may hold values from -0.375 to 0.375
- w_out: bfloat16 [512, 256], replicated, may hold values from -0.25 to 0.25
Outputs:
- grid_out: bfloat16 [768, 1440, 256], P('lat', 'chan')
- spectrum: bfloat16 [384, 721, 2, 256], P('lat', None, None, 'chan')
The draws below stay inside these ranges and needn't reach their ends.
Inputs may be any that keep to these rules, and one draw needn't show every extreme that they name: `pairing`: each value 0 to 359 stands in exactly one slot; every other slot holds -1; slot s belongs to lat device s // 12. offsets[0] = 0, offsets[32] = 384, offsets never fall, offsets[d] differs from d * 12 by at most 6, and some band holds exactly 24 latitudes.
All inputs are finite; a program needn't handle non-finite values.
Results may differ from the reference program's by a relative error of at most 0.013.
Values may be sent and summed in bfloat16 or wider, within the bound.
A program may use at most 256 MiB of HBM per device.

```python
import math
import jax
import jax.numpy as jnp
from jax import lax

C = 256
HID = 512
NLON = 1440
L = 720
LAT_DEV = 12
LAT_CAP = 24
NLAT = 384
NPAIR = 360
SLOTS = 12
KP = 721
N_LAT = 32


def draw_offsets(key, part):
    key = jax.random.fold_in(key, 11)
    device_count = NLAT // LAT_DEV
    half_band = LAT_DEV // 2
    first_key, second_key = jax.random.split(key)
    shifts = jax.random.randint(first_key, (device_count + 1,), -half_band, half_band + 1)
    marked = jax.random.randint(second_key, (), 1, device_count - 1)
    places = jnp.arange(device_count + 1, dtype=jnp.int32)
    shifts = jnp.where(places == marked, -half_band, shifts)
    shifts = jnp.where(places == marked + 1, half_band, shifts)
    shifts = jnp.where((places == 0) | (places == device_count), 0, shifts)
    return (places * LAT_DEV + shifts).astype(jnp.int32)


def draw_pairing(key, part):
    key = jax.random.fold_in(key, 23)
    slot_total = NLAT // LAT_DEV * SLOTS
    shuffled = jax.random.permutation(key, slot_total)
    return jnp.where(shuffled < NPAIR, shuffled, -1).astype(jnp.int32)


def level_of(stream_key, dims, cuts, smallest, high):
    factor_of, own = 1.0, jax.random.fold_in(stream_key, 6)
    for dim, blocks in cuts:
        steps = jnp.exp(jax.random.uniform(jax.random.fold_in(own, dim), (blocks,), jnp.float32, smallest / len(cuts), high / len(cuts)))
        factor_of = factor_of * jnp.repeat(steps, dims[dim] // blocks).reshape([-1 if axis == dim else 1 for axis in range(len(dims))])
    return factor_of


def noise(own_key, shape, spread, reach, cuts=(), held_as=jnp.bfloat16):
    loudness = level_of(own_key, shape, cuts, -0.22, 0.18) if cuts else 1.0
    array = jax.random.normal(own_key, shape, jnp.float32) * spread * loudness
    return jnp.minimum(jnp.maximum(array, -reach), reach).astype(held_as)


def setup_inputs(seed: int = 0) -> dict:
    key_list = jax.random.split(jax.random.key(seed), 8)
    return {
        "grid_in": noise(key_list[0], (N_LAT * LAT_CAP, NLON, C), 1.0, 6.0, ((0, 32), (2, 8))),
        "pairing": draw_pairing(jax.random.fold_in(key_list[7], 71), 0),
        "offsets": draw_offsets(jax.random.fold_in(key_list[7], 71), 0),
        "legendre": noise(key_list[3], (N_LAT * SLOTS, KP, NLAT), NLAT ** -0.5, 0.3125, ((0, 32),)),
        "degree_mix": noise(key_list[4], (L, C, C), C ** -0.5, 0.375, ((1, 32), (2, 8))),
        "w_in": noise(key_list[5], (C, HID), C ** -0.5, 0.375),
        "w_out": noise(key_list[6], (HID, C), HID ** -0.5, 0.25),
    }


def forward_table(lon_count, order_count):
    lon_index = jnp.arange(lon_count, dtype=jnp.int32)
    order_index = jnp.arange(order_count, dtype=jnp.int32)
    phases = (lon_index[:, None] * order_index[None, :] % lon_count).astype(jnp.float32) * (2.0 * math.pi / lon_count)
    factor = 1.0 / math.sqrt(lon_count)
    return jnp.concatenate([jnp.cos(phases) * factor, -jnp.sin(phases) * factor], axis=1).astype(jnp.bfloat16)

def inverse_table(lon_count, order_count):
    lon_index = jnp.arange(lon_count, dtype=jnp.int32)
    order_index = jnp.arange(order_count, dtype=jnp.int32)
    phases = (lon_index[:, None] * order_index[None, :] % lon_count).astype(jnp.float32) * (2.0 * math.pi / lon_count)
    factor = 1.0 / math.sqrt(lon_count)
    weights = jnp.where(order_index == 0, 1.0, 2.0).astype(jnp.float32)[:, None] * factor
    return jnp.concatenate([jnp.cos(phases).T * weights, -jnp.sin(phases).T * weights], axis=0).astype(jnp.bfloat16)

def order_sources(pairing, degrees):
    orders = jnp.arange(degrees, dtype=jnp.int32)
    partner = degrees - 1 - orders
    lower = jnp.minimum(orders, partner)
    upper_side = (orders > partner).astype(jnp.int32)
    slot_ids = jnp.arange(pairing.shape[0], dtype=jnp.int32)
    owner_slot = lax.optimization_barrier(jnp.sum(jnp.where(pairing[None, :] == lower[:, None], slot_ids[None, :], 0), axis=1))
    return (owner_slot * 2 + upper_side).astype(jnp.int32)

def per_slot_take(values, indices):
    return jax.vmap(lambda source_block, pick_index: jnp.take(source_block, pick_index, axis=0))(values, indices)

def low_mask(first, packed):
    degrees = packed - 1
    packed_index = jnp.arange(packed, dtype=jnp.int32)
    base = jnp.maximum(first, 0)
    return (packed_index[None, :] < degrees - base[:, None])[:, :, None, None]

def mix_degrees(coeffs, first, weight):
    slot_count, packed, _, in_width = coeffs.shape
    degrees = packed - 1
    base = jnp.maximum(first, 0)
    degree_index = jnp.arange(degrees, dtype=jnp.int32)
    packed_index = jnp.arange(packed, dtype=jnp.int32)
    low_index = jnp.clip(degree_index[None, :] - base[:, None], 0, degrees).astype(jnp.int32)
    side_low = per_slot_take(coeffs, low_index)
    side_high = coeffs[:, 1:]
    stacked = jnp.stack([side_low, side_high], axis=1)
    operand = jnp.transpose(stacked, (2, 0, 1, 3, 4)).reshape(degrees, slot_count * 4, in_width)
    result = jnp.einsum('lri,lio->lro', operand.astype(jnp.float32), weight.astype(jnp.float32))
    out_width = result.shape[2]
    result = jnp.transpose(result.reshape(degrees, slot_count, 2, 2, out_width), (1, 2, 0, 3, 4))
    pick_low = per_slot_take(result[:, 0], jnp.clip(base[:, None] + packed_index[None, :], 0, degrees - 1).astype(jnp.int32))
    pick_high = jnp.take(result[:, 1], jnp.clip(packed_index - 1, 0, degrees - 1).astype(jnp.int32), axis=1)
    mixed = jnp.where(low_mask(first, packed), pick_low, pick_high)
    return jnp.where((first >= 0)[:, None, None, None], mixed, jnp.float32(0.0))

def pointwise(state, w_in, w_out):
    values = state.astype(jnp.float32)
    centered = values - lax.optimization_barrier(jnp.mean(values, axis=-1, keepdims=True))
    normed = (centered * lax.rsqrt(lax.optimization_barrier(jnp.mean(centered * centered, axis=-1, keepdims=True)) + 1e-05)).astype(jnp.bfloat16)
    hidden = jax.nn.gelu(jnp.dot(normed, w_in, preferred_element_type=jnp.float32), approximate=True).astype(jnp.bfloat16)
    return (values + jnp.dot(hidden, w_out, preferred_element_type=jnp.float32)).astype(jnp.bfloat16)

def reference(grid_in, pairing, offsets, legendre, degree_mix, w_in, w_out):
    slot_total = N_LAT * SLOTS
    global_lat = jnp.arange(NLAT, dtype=jnp.int32)
    owners = lax.optimization_barrier(jnp.sum((offsets[None, 1:N_LAT] <= global_lat[:, None]).astype(jnp.int32), axis=1))
    sources = (owners * LAT_CAP + global_lat - jnp.take(offsets, owners)).astype(jnp.int32)
    grid = jnp.take(grid_in, sources, axis=0)
    spectra = jnp.einsum('gnc,nk->gkc', grid.astype(jnp.float32), forward_table(NLON, L).astype(jnp.float32)).astype(jnp.bfloat16)
    spectra = spectra.reshape(NLAT, 2, L, C)
    base_all = jnp.maximum(pairing, 0)
    wanted = jnp.stack([base_all, L - 1 - base_all], axis=1).reshape(-1).astype(jnp.int32)
    picked = jnp.take(spectra, wanted, axis=2)
    live = jnp.repeat(pairing >= 0, 2)
    picked = jnp.where(live[None, None, :, None], picked, jnp.bfloat16(0.0))
    picked = jnp.transpose(picked, (0, 2, 1, 3)).reshape(NLAT, N_LAT, SLOTS, 4 * C)
    picked = jnp.transpose(picked, (1, 0, 2, 3))
    weight32 = degree_mix.astype(jnp.float32)

    def one_group(item):
        table, latitudes, first = item
        both = jnp.einsum('skg,gsy->sky', table.astype(jnp.float32), latitudes.astype(jnp.float32))
        both = both.reshape(SLOTS, KP, 2, 2, C)
        is_low = low_mask(first, KP)
        coeffs = jnp.where(is_low, both[:, :, 0], both[:, :, 1])
        coeffs = jnp.where((first >= 0)[:, None, None, None], coeffs, jnp.float32(0.0)).astype(jnp.bfloat16)
        mixed = mix_degrees(coeffs, first, weight32).astype(jnp.bfloat16)
        zeros = jnp.zeros_like(mixed)
        split = jnp.stack([jnp.where(is_low, mixed, zeros), jnp.where(is_low, zeros, mixed)], axis=2)
        back = jnp.einsum('skg,sky->gsy', table.astype(jnp.float32), split.reshape(SLOTS, KP, 4 * C).astype(jnp.float32))
        return (mixed, back.astype(jnp.bfloat16))
    mixed_all, back_all = lax.map(one_group, (legendre.reshape(N_LAT, SLOTS, KP, NLAT), picked, pairing.reshape(N_LAT, SLOTS)))
    spectrum = mixed_all.reshape(slot_total, KP, 2, C)
    back_all = jnp.transpose(back_all, (1, 0, 2, 3)).reshape(NLAT, slot_total * 2, 2, C)
    ordered = jnp.take(back_all, order_sources(pairing, L), axis=1)
    ordered = jnp.transpose(ordered, (0, 2, 1, 3)).reshape(NLAT, 2 * L, C)
    filtered = jnp.einsum('gkc,kn->gnc', ordered.astype(jnp.float32), inverse_table(NLON, L).astype(jnp.float32))
    state = (grid.astype(jnp.float32) + filtered).astype(jnp.bfloat16)
    result = pointwise(state, w_in, w_out)
    padded_index = jnp.arange(N_LAT * LAT_CAP, dtype=jnp.int32)
    owner_of_row = padded_index // LAT_CAP
    within = padded_index % LAT_CAP
    row_lat = jnp.take(offsets, owner_of_row) + within
    valid = within < jnp.take(offsets, owner_of_row + 1) - jnp.take(offsets, owner_of_row)
    gathered = jnp.take(result, jnp.clip(row_lat, 0, NLAT - 1).astype(jnp.int32), axis=0)
    grid_out = jnp.where(valid[:, None, None], gathered, jnp.bfloat16(0.0))
    return (grid_out, spectrum)
```

```python
import functools
import math

import jax
import jax.numpy as jnp
import ml_dtypes
import numpy as np
from jax import lax
from jax.experimental import pallas as pl
from jax.experimental.pallas import tpu as pltpu
from jax.sharding import Mesh
from jax.sharding import PartitionSpec as P

NLON = 1440
L = 720
KP = 721
SLOTS = 12
ROWS = 12
HALO = 6
CW = 32
NCH = 8
NY = 4
NZ = 8
NLATD = 32
CHUNK = 180
CHUNKP = 192
NPADDED = NCH * CHUNKP
JO = 12
JR = JO + 1
MROWS = 160
F32 = jnp.float32
BF16 = jnp.bfloat16
VMEM_LIMIT = 56 * 1024 * 1024


def forward_table():
    n = np.arange(NLON, dtype=np.int64)
    m = np.arange(L, dtype=np.int64)
    ph = ((m[:, None] * n[None, :]) % NLON).astype(np.float32) * np.float32(2.0 * math.pi / NLON)
    f = np.float32(1.0 / math.sqrt(NLON))
    table = np.concatenate([np.cos(ph) * f, -np.sin(ph) * f], axis=0)
    return table.astype(ml_dtypes.bfloat16)


def inverse_table():
    n = np.arange(NLON, dtype=np.int64)
    m = np.arange(L, dtype=np.int64)
    ph = ((n[:, None] * m[None, :]) % NLON).astype(np.float32) * np.float32(2.0 * math.pi / NLON)
    f = np.float32(1.0 / math.sqrt(NLON))
    w = np.where(m == 0, 1.0, 2.0).astype(np.float32)[None, :] * f
    table = np.concatenate([np.cos(ph) * w, -np.sin(ph) * w], axis=1)
    padded = np.zeros((NCH, CHUNKP, 2 * L), np.float32)
    padded[:, :CHUNK] = table.reshape(NCH, CHUNK, 2 * L)
    return padded.reshape(NPADDED, 2 * L).astype(ml_dtypes.bfloat16)


def pad_rows():
    sel = np.zeros((NCH, CHUNKP, NLON), np.float32)
    for c in range(NCH):
        for i in range(CHUNK):
            sel[c, i, c * CHUNK + i] = 1.0
    return sel.reshape(NPADDED, NLON).astype(ml_dtypes.bfloat16)


def degree_order():
    sel = np.zeros((32, 2 * JO, L), np.float32)
    for o in range(L // 2 // JO):
        for jj in range(JO):
            j = o * JO + jj
            sel[o, jj, j] = 1.0
            sel[o, JO + jj, L - 1 - j] = 1.0
    return sel.reshape(32 * 2 * JO, L).astype(ml_dtypes.bfloat16)


def swap4(v):
    lane = lax.broadcasted_iota(jnp.int32, v[0].shape, 1)
    lo = lane < 64
    even = (lane // 32) % 2 == 0
    r = [pltpu.roll(x, 64, 1) for x in v]
    a0 = jnp.where(lo, v[0], r[2])
    a2 = jnp.where(lo, r[0], v[2])
    a1 = jnp.where(lo, v[1], r[3])
    a3 = jnp.where(lo, r[1], v[3])
    o0 = jnp.where(even, a0, pltpu.roll(a1, 32, 1))
    o1 = jnp.where(even, pltpu.roll(a0, 96, 1), a1)
    o2 = jnp.where(even, a2, pltpu.roll(a3, 32, 1))
    o3 = jnp.where(even, pltpu.roll(a2, 96, 1), a3)
    return [o0, o1, o2, o3]


def pair_one_hots(base):
    ri = lax.broadcasted_iota(jnp.int32, (32 * JR, 1), 0)
    jj = ri // 32
    o = ri % 32
    j = JO * o + jj
    regular = (jj < JO) & (j < L // 2)
    extra = (jj == JO) & (base // JO == o)
    kx = jnp.where(regular, L - 1 - base - j, jnp.where(extra, L - base, -1))
    ky = jnp.where(regular, jnp.where(j >= base, j - base, L - j), -1)
    col = lax.broadcasted_iota(jnp.int32, (32 * JR, KP), 1)
    sx = jnp.where(col == kx, 1.0, 0.0).astype(BF16)
    sy = jnp.where(col == ky, 1.0, 0.0).astype(BF16)
    return sx, sy


def legendre_kernel(first_ref, inc_ref, leg_ref, out_ref, scr_f, scr_r, scr_o):
    s = pl.program_id(0)

    @pl.when(s == 0)
    def _():
        for rg in range(3):
            scr_f[rg] = inc_ref[:, rg * 128 : rg * 128 + 128].astype(F32)
        scr_o[...] = jnp.zeros_like(scr_o)

    for rg in range(3):
        t = [scr_f.at[rg][pl.ds(q * SLOTS + s, 32, stride=48), :] for q in range(4)]
        for r4, u in enumerate(swap4(t)):
            scr_r[pl.ds(rg * 4 + r4, 32, stride=ROWS), :] = u
    both = jnp.dot(leg_ref[0], scr_r[...].astype(BF16), preferred_element_type=F32)
    base = jnp.maximum(first_ref[s], 0)
    kio = lax.broadcasted_iota(jnp.int32, both.shape, 0)
    lane = lax.broadcasted_iota(jnp.int32, both.shape, 1)
    low = jnp.where(kio < L - base, 1, 0)
    left = jnp.where(lane < 64, 1, 0)
    twice = jnp.where(low == left, both, pltpu.roll(both, 64, 1)).astype(BF16)
    sx, sy = pair_one_hots(base)
    qx = jnp.dot(sx, twice, preferred_element_type=F32)
    qy = jnp.dot(sy, twice, preferred_element_type=F32)
    lane2 = lax.broadcasted_iota(jnp.int32, qx.shape, 1)
    q = jnp.where(lane2 < 64, qx, qy)
    for jj in range(JR):
        scr_o[pl.ds(s * JR + jj, 32, stride=MROWS), :] = q[jj * 32 : jj * 32 + 32]

    @pl.when(s == SLOTS - 1)
    def _():
        out_ref[...] = scr_o[...].astype(BF16)


def run_legendre(first, incoming, legendre):
    return pl.pallas_call(
        legendre_kernel,
        grid_spec=pltpu.PrefetchScalarGridSpec(
            num_scalar_prefetch=1,
            grid=(SLOTS,),
            in_specs=[
                pl.BlockSpec((NLATD * 48, ROWS * CW), lambda s, f: (0, 0)),
                pl.BlockSpec((1, KP, NLATD * ROWS), lambda s, f: (s, 0, 0)),
            ],
            out_specs=pl.BlockSpec((32 * MROWS, 128), lambda s, f: (0, 0)),
            scratch_shapes=[
                pltpu.VMEM((3, NLATD * 48, 128), F32),
                pltpu.VMEM((NLATD * ROWS, 128), F32),
                pltpu.VMEM((32 * MROWS, 128), F32),
            ],
        ),
        out_shape=jax.ShapeDtypeStruct((32 * MROWS, 128), BF16),
        compiler_params=pltpu.CompilerParams(vmem_limit_bytes=VMEM_LIMIT),
        name="legendre_forward",
    )(first, incoming, legendre)


def weights_kernel(w_ref, out_ref, scr):
    for y in range(NY):
        for h in range(2):
            for ih in range(2):
                t = [
                    w_ref[0, y * 8 + h * 4 + c, :, ih * 128 : ih * 128 + 128].astype(F32)
                    for c in range(4)
                ]
                for i4, u in enumerate(swap4(t)):
                    scr.at[h][pl.ds(y * 8 + ih * 4 + i4, 2 * JO, stride=32), :] = u
    for h in range(2):
        out_ref[:, :, 0, :, h * 128 : h * 128 + 128] = scr[h].astype(BF16).reshape(2 * JO, NY, 8, 128)


def run_weights(gathered):
    return pl.pallas_call(
        weights_kernel,
        grid=(NZ,),
        in_specs=[pl.BlockSpec((1, 32, 2 * JO, 256), lambda z: (z, 0, 0, 0))],
        out_specs=pl.BlockSpec((2 * JO, NY, 1, 8, 256), lambda z: (0, 0, z, 0, 0)),
        scratch_shapes=[pltpu.VMEM((2, 2 * JO * 32, 128), F32)],
        out_shape=jax.ShapeDtypeStruct((2 * JO, NY, NZ, 8, 256), BF16),
        compiler_params=pltpu.CompilerParams(vmem_limit_bytes=VMEM_LIMIT),
        name="unpack_weights",
    )(gathered)


VROWS = NY * MROWS


def mix_kernel(owner_ref, d_ref, w_ref, a_ref, out_ref, v, ex):
    for y in range(NY):
        for h in range(2):
            t = [d_ref[y * 8 + h * 4 + i].astype(F32) for i in range(4)]
            for q, u in enumerate(swap4(t)):
                v[h, q * VROWS + y * MROWS : q * VROWS + (y + 1) * MROWS, :] = u
    v[:, 4 * VROWS :, :] = jnp.zeros((2, v.shape[1] - 4 * VROWS, 128), F32)
    lane_a = a_ref[...]

    def rows(q, jj):
        return jnp.concatenate(
            [
                jnp.concatenate(
                    [v.at[h][pl.ds(start, 16, stride=JR), :] for h in range(2)], axis=1
                )
                for start in (q * VROWS + y * MROWS + jj for y in range(NY))
            ],
            axis=0,
        )

    extra = jnp.concatenate([rows(0, JO), rows(1, JO)], axis=0).astype(BF16)
    ex[...] = jnp.zeros_like(ex)
    owner = owner_ref[0]

    def put(q, jj, value):
        for y in range(NY):
            start = q * VROWS + y * MROWS + jj
            for h in range(2):
                v.at[h][pl.ds(start, SLOTS, stride=JR), :] = value[
                    y * 16 : y * 16 + SLOTS, h * 128 : h * 128 + 128
                ]

    for jj in range(JO):
        j = owner * JO + jj
        x = jnp.concatenate([rows(0, jj), rows(1, jj)], axis=0).astype(BF16)
        yv = jnp.concatenate([rows(2, jj), rows(3, jj)], axis=0).astype(BF16)
        upper = jnp.dot(
            jnp.concatenate([x, yv, extra], axis=0), w_ref[JO + jj], preferred_element_type=F32
        )
        lower = jnp.dot(yv, w_ref[jj], preferred_element_type=F32)
        ym = jnp.where(lane_a <= j, lower, upper[128:256])
        ex[...] += jnp.where(lane_a == j, upper[256:384], 0.0)
        put(0, jj, upper[0:64])
        put(1, jj, upper[64:128])
        put(2, jj, ym[0:64])
        put(3, jj, ym[64:128])
    put(0, JO, ex[0:64, :])
    put(1, JO, ex[64:128, :])
    for y in range(NY):
        for h in range(2):
            t = [
                v[h, q * VROWS + y * MROWS : q * VROWS + (y + 1) * MROWS, :]
                for q in range(4)
            ]
            for i, u in enumerate(swap4(t)):
                out_ref[y * 8 + h * 4 + i] = u.astype(BF16)


def run_mix(owner, coeffs, weights, lower_orders):
    return pl.pallas_call(
        mix_kernel,
        in_specs=[
            pl.BlockSpec(memory_space=pltpu.SMEM),
            pl.BlockSpec(memory_space=pltpu.VMEM),
            pl.BlockSpec(memory_space=pltpu.VMEM),
            pl.BlockSpec(memory_space=pltpu.VMEM),
        ],
        out_specs=pl.BlockSpec(memory_space=pltpu.VMEM),
        scratch_shapes=[pltpu.VMEM((2, 4 * VROWS + 64, 128), F32), pltpu.VMEM((128, 256), F32)],
        out_shape=jax.ShapeDtypeStruct((32, MROWS, 128), BF16),
        compiler_params=pltpu.CompilerParams(vmem_limit_bytes=VMEM_LIMIT),
        name="mix_degrees",
    )(owner, coeffs, weights, lower_orders)


def inverse_kernel(first_ref, d_ref, leg_ref, spec_ref, out_ref, scr_f, scr_b, scr_e):
    s = pl.program_id(0)

    @pl.when(s == 0)
    def _():
        scr_f[...] = d_ref[...].astype(F32)

    q = jnp.concatenate(
        [scr_f[pl.ds(s * JR + jj, 32, stride=MROWS), :] for jj in range(JR)], axis=0
    )
    qt = jnp.transpose(q).astype(BF16)
    base = jnp.maximum(first_ref[s], 0)
    sx, sy = pair_one_hots(base)
    ct = jnp.dot(qt[0:64], sx, preferred_element_type=F32) + jnp.dot(
        qt[64:128], sy, preferred_element_type=F32
    )
    spec_ref[0] = ct.astype(BF16)
    low = lax.broadcasted_iota(jnp.int32, ct.shape, 1) < L - base
    split = jnp.concatenate([jnp.where(low, ct, 0.0), jnp.where(low, 0.0, ct)], axis=0).astype(BF16)
    back = jnp.dot(split, leg_ref[0], preferred_element_type=F32)
    scr_b[...] = jnp.transpose(back)
    for rg in range(3):
        t = [scr_b[pl.ds(rg * 4 + r4, 32, stride=ROWS), :] for r4 in range(4)]
        for qi, u in enumerate(swap4(t)):
            scr_e.at[rg][pl.ds(qi * SLOTS + s, 32, stride=48), :] = u

    @pl.when(s == SLOTS - 1)
    def _():
        for rg in range(3):
            out_ref[:, rg * 128 : rg * 128 + 128] = scr_e[rg].astype(BF16)


def run_inverse(first, mixed, legendre):
    return pl.pallas_call(
        inverse_kernel,
        grid_spec=pltpu.PrefetchScalarGridSpec(
            num_scalar_prefetch=1,
            grid=(SLOTS,),
            in_specs=[
                pl.BlockSpec((32 * MROWS, 128), lambda s, f: (0, 0)),
                pl.BlockSpec((1, KP, NLATD * ROWS), lambda s, f: (s, 0, 0)),
            ],
            out_specs=[
                pl.BlockSpec((1, 2 * CW, KP), lambda s, f: (s, 0, 0)),
                pl.BlockSpec((NLATD * 48, ROWS * CW), lambda s, f: (0, 0)),
            ],
            scratch_shapes=[
                pltpu.VMEM((32 * MROWS, 128), F32),
                pltpu.VMEM((NLATD * ROWS, 128), F32),
                pltpu.VMEM((3, NLATD * 48, 128), F32),
            ],
        ),
        out_shape=[
            jax.ShapeDtypeStruct((SLOTS, 2 * CW, KP), BF16),
            jax.ShapeDtypeStruct((NLATD * 48, ROWS * CW), BF16),
        ],
        compiler_params=pltpu.CompilerParams(vmem_limit_bytes=VMEM_LIMIT),
        name="legendre_inverse",
    )(first, mixed, legendre)


def mlp_kernel(f_ref, w_in_ref, w_out_ref, out_ref, v):
    for h in range(2):
        t = [f_ref[h * 4 + i].astype(F32) for i in range(4)]
        for r4, u in enumerate(swap4(t)):
            v[r4, :, h * 128 : h * 128 + 128] = u
    for r4 in range(4):
        values = v[r4]
        centered = values - jnp.mean(values, axis=-1, keepdims=True)
        normed = (
            centered * lax.rsqrt(jnp.mean(centered * centered, axis=-1, keepdims=True) + 1e-05)
        ).astype(BF16)
        hidden = jax.nn.gelu(
            jnp.dot(normed, w_in_ref[...], preferred_element_type=F32), approximate=True
        ).astype(BF16)
        out_ref[r4] = (
            values + jnp.dot(hidden, w_out_ref[...], preferred_element_type=F32)
        ).astype(BF16)


def run_mlp(relaid, w_in, w_out):
    return pl.pallas_call(
        mlp_kernel,
        grid=(3,),
        in_specs=[
            pl.BlockSpec((NCH, CHUNKP, 128), lambda r: (0, 0, r)),
            pl.BlockSpec((256, 512), lambda r: (0, 0)),
            pl.BlockSpec((512, 256), lambda r: (0, 0)),
        ],
        out_specs=pl.BlockSpec((4, CHUNKP, 256), lambda r: (r, 0, 0)),
        scratch_shapes=[pltpu.VMEM((4, CHUNKP, 256), F32)],
        out_shape=jax.ShapeDtypeStruct((ROWS, CHUNKP, 256), BF16),
        compiler_params=pltpu.CompilerParams(vmem_limit_bytes=VMEM_LIMIT),
        name="pointwise",
    )(relaid, w_in, w_out)


def order_one_hot(pairing):
    a = pairing.reshape(NLATD, 1, 1, SLOTS)
    order = jnp.concatenate([a, L - 1 - a], axis=1)
    part = jnp.arange(2, dtype=jnp.int32).reshape(1, 1, 2, 1)
    col = jnp.where(a >= 0, part * L + order, -1).reshape(-1)
    return (col[:, None] == jnp.arange(2 * L, dtype=jnp.int32)[None, :]).astype(BF16)


def dot_nt(a, b):
    return lax.dot_general(a, b, (((1,), (1,)), ((), ())), preferred_element_type=F32)


def per_device(grid_in, pairing, offsets, legendre, degree_mix, w_in, w_out):
    lat = ("y", "z")
    me = lax.axis_index("y") * NZ + lax.axis_index("z")
    chan = lax.axis_index("chan")
    start = jnp.take(offsets, me)
    length = jnp.take(offsets, me + 1) - start
    first = lax.dynamic_slice_in_dim(pairing, me * SLOTS, SLOTS)
    cap = grid_in.shape[0]
    to_right = [(i, i + 1) for i in range(NLATD - 1)]
    to_left = [(i + 1, i) for i in range(NLATD - 1)]

    rows = jnp.transpose(grid_in, (0, 2, 1))
    valid = (jnp.arange(cap, dtype=jnp.int32) < length)[:, None, None]
    rows = jnp.where(valid, rows, jnp.zeros((), BF16))
    shift = me * ROWS - HALO - start
    rows = jnp.concatenate([jnp.zeros((12, CW, NLON), BF16), rows], axis=0)
    virt = lax.dynamic_slice_in_dim(rows, 12 + shift, cap, axis=0)
    from_right = lax.ppermute(virt[:HALO], lat, to_left)
    from_left = lax.ppermute(virt[HALO + ROWS :], lat, to_right)
    own = virt[HALO : HALO + ROWS]
    xt = (own + jnp.concatenate([from_left, from_right], axis=0)).reshape(ROWS * CW, NLON)

    by_degree = dot_nt(
        jnp.asarray(degree_order()),
        jnp.transpose(degree_mix, (1, 2, 0)).reshape(8 * CW, L),
    ).astype(BF16)
    owned = lax.all_to_all(
        by_degree.reshape(32, 2 * JO, 256), ("y", "chan"), split_axis=0, concat_axis=0, tiled=True
    )
    gathered = lax.all_gather(owned, "z", axis=0, tiled=False)
    weights = run_weights(gathered)
    weights = weights.reshape(2 * JO, 256, 256)

    picks = order_one_hot(pairing)
    forward = jnp.dot(picks, jnp.asarray(forward_table()), preferred_element_type=F32).astype(BF16)
    inverse = dot_nt(jnp.asarray(inverse_table()), picks).astype(BF16)

    spectra = dot_nt(forward, xt).astype(BF16).reshape(NLATD, 48, ROWS * CW)
    incoming = lax.all_to_all(spectra, lat, split_axis=0, concat_axis=0, tiled=True)
    coeffs = run_legendre(first, incoming.reshape(NLATD * 48, ROWS * CW), legendre)
    at_owner = lax.all_to_all(
        coeffs.reshape(32, MROWS, 128), ("y", "chan"), split_axis=0, concat_axis=0, tiled=True
    )
    owner = (lax.axis_index("y") * NCH + chan).reshape(1)
    z = lax.axis_index("z")
    a_here = lax.dynamic_slice_in_dim(pairing.reshape(NY, NZ, SLOTS), z, 1, axis=1)[:, 0]
    a_here = jnp.concatenate([a_here, jnp.full((NY, 4), -1, jnp.int32)], axis=1).reshape(1, NY * 16)
    a_here = jnp.broadcast_to(a_here, (2, NY * 16)).reshape(128, 1)
    mixed = run_mix(owner, at_owner, weights, a_here)
    returned = lax.all_to_all(mixed, ("y", "chan"), split_axis=0, concat_axis=0, tiled=True)
    spectrum, back = run_inverse(first, returned.reshape(32 * MROWS, 128), legendre)
    spectrum = jnp.transpose(spectrum.reshape(SLOTS, 2, CW, KP), (0, 3, 1, 2))
    homeward = lax.all_to_all(
        back.reshape(NLATD, 48, ROWS * CW), lat, split_axis=0, concat_axis=0, tiled=True
    ).reshape(NLATD * 48, ROWS * CW)
    padded = dot_nt(jnp.asarray(pad_rows()), xt)
    state = (padded + jnp.dot(inverse, homeward, preferred_element_type=F32)).astype(BF16)
    relaid = lax.all_to_all(
        state.reshape(NCH, CHUNKP, ROWS * CW), "chan", split_axis=0, concat_axis=0, tiled=True
    )
    result = run_mlp(relaid, w_in, w_out)[:, :CHUNK]
    out_right = lax.ppermute(result[:HALO], lat, to_left)
    out_left = lax.ppermute(result[HALO:], lat, to_right)
    virt_out = jnp.concatenate([out_left, result, out_right, jnp.zeros((12, CHUNK, 256), BF16)], axis=0)
    picked = lax.dynamic_slice_in_dim(virt_out, -shift, cap, axis=0)
    grid_out = jnp.where(valid, picked, jnp.zeros((), BF16))
    return (grid_out, spectrum)


def solution(mesh):
    fine = Mesh(np.asarray(mesh.devices).reshape(NY, NZ, NCH), ("y", "z", "chan"))
    lat = ("y", "z")
    in_specs = (
        P(lat, None, "chan"),
        P(),
        P(),
        P(lat, None, None),
        P(None, lat, "chan"),
        P(),
        P(),
    )
    out_specs = (P(lat, "chan", None), P(lat, None, None, "chan"))
    return jax.shard_map(per_device, mesh=fine, in_specs=in_specs, out_specs=out_specs, check_vma=False)
```

```python
import functools
import math

import jax
import jax.numpy as jnp
import ml_dtypes
import numpy as np
from jax import lax
from jax.experimental import pallas as pl
from jax.experimental.pallas import tpu as pltpu
from jax.sharding import Mesh
from jax.sharding import PartitionSpec as P

NLON = 1440
L = 720
KP = 721
SLOTS = 12
ROWS = 12
HALO = 6
CW = 32
NCH = 8
NY = 4
NZ = 8
NLATD = 32
CHUNK = 180
CHUNKP = 192
NPADDED = NCH * CHUNKP
JO = 12
JR = JO + 1
ENTRIES = 32 * JR
MROWS = 160
SG = 4
NSG = SLOTS // SG
EROWS = 2 * SG
F32 = jnp.float32
BF16 = jnp.bfloat16
VMEM_LIMIT = 56 * 1024 * 1024


def forward_table():
    n = np.arange(NLON, dtype=np.int64)
    m = np.arange(L, dtype=np.int64)
    ph = ((m[:, None] * n[None, :]) % NLON).astype(np.float32) * np.float32(2.0 * math.pi / NLON)
    f = np.float32(1.0 / math.sqrt(NLON))
    table = np.concatenate([np.cos(ph) * f, -np.sin(ph) * f], axis=0)
    return table.astype(ml_dtypes.bfloat16)


def inverse_table():
    n = np.arange(NLON, dtype=np.int64)
    m = np.arange(L, dtype=np.int64)
    ph = ((n[:, None] * m[None, :]) % NLON).astype(np.float32) * np.float32(2.0 * math.pi / NLON)
    f = np.float32(1.0 / math.sqrt(NLON))
    w = np.where(m == 0, 1.0, 2.0).astype(np.float32)[None, :] * f
    table = np.concatenate([np.cos(ph) * w, -np.sin(ph) * w], axis=1)
    padded = np.zeros((NCH, CHUNKP, 2 * L), np.float32)
    padded[:, :CHUNK] = table.reshape(NCH, CHUNK, 2 * L)
    return padded.reshape(NPADDED, 2 * L).astype(ml_dtypes.bfloat16)


def pad_rows():
    sel = np.zeros((NCH, CHUNKP, NLON), np.float32)
    for c in range(NCH):
        for i in range(CHUNK):
            sel[c, i, c * CHUNK + i] = 1.0
    return sel.reshape(NPADDED, NLON).astype(ml_dtypes.bfloat16)


def degree_order():
    sel = np.zeros((32, 2 * JO, L), np.float32)
    for o in range(L // 2 // JO):
        for jj in range(JO):
            j = o * JO + jj
            sel[o, jj, j] = 1.0
            sel[o, JO + jj, L - 1 - j] = 1.0
    return sel.reshape(32 * 2 * JO, L).astype(ml_dtypes.bfloat16)


def swap_table():
    sel = np.zeros((4, 4, CW, 4, 4, CW), np.float32)
    for q in range(4):
        for r in range(4):
            for c in range(CW):
                sel[q, r, c, r, q, c] = 1.0
    return sel.reshape(512, 512).astype(ml_dtypes.bfloat16)


def swap_mirror_table():
    base = swap_table().reshape(512, 4, 4, CW)
    return np.concatenate([base, base[:, :, [2, 3, 0, 1]]], axis=2).reshape(512, 1024)


def swap4(v, table):
    joined = jnp.concatenate([x.astype(BF16) for x in v], axis=1)
    out = jnp.dot(joined, table, preferred_element_type=F32)
    width = out.shape[1] // 4
    return [out[:, k * width : (k + 1) * width] for k in range(4)]


def pair_one_hots(base):
    ri = lax.broadcasted_iota(jnp.int32, (32 * JR, 1), 0)
    jj = ri // 32
    o = ri % 32
    j = JO * o + jj
    regular = (jj < JO) & (j < L // 2)
    extra = (jj == JO) & (base // JO == o)
    kx = jnp.where(regular, L - 1 - base - j, jnp.where(extra, L - base, -1))
    ky = jnp.where(regular, jnp.where(j >= base, j - base, L - j), -1)
    col = lax.broadcasted_iota(jnp.int32, (32 * JR, KP), 1)
    sx = jnp.where(col == kx, 1.0, 0.0).astype(BF16)
    sy = jnp.where(col == ky, 1.0, 0.0).astype(BF16)
    return sx, sy


def legendre_kernel(first_ref, inc_ref, leg_ref, swap_ref, out_ref, scr_f, scr_r, scr_o):
    group = pl.program_id(0)

    @pl.when(group == 0)
    def _():
        for k in range(6):
            scr_f[k] = inc_ref[:, k * 128 : k * 128 + 128].astype(F32)
        scr_o[...] = jnp.zeros_like(scr_o)

    row = lax.broadcasted_iota(jnp.int32, (ENTRIES, 128), 0)
    lane = lax.broadcasted_iota(jnp.int32, (ENTRIES, 128), 1)
    degree = JO * (row % 32) + row // 32
    for ss in range(SG):
        s = group * SG + ss
        t = [
            jnp.concatenate(
                [
                    scr_f.at[p * 3 + rg][pl.ds(side * SLOTS + s, 32, stride=24), :]
                    for rg in range(3)
                ],
                axis=0,
            )
            for side in range(2)
            for p in range(2)
        ]
        for r4, u in enumerate(swap4(t, swap_ref[...])):
            for rg in range(3):
                for k in range(2):
                    scr_r.at[ss * 2 + k][pl.ds(rg * 4 + r4, 32, stride=ROWS), :] = u[
                        rg * 32 : rg * 32 + 32, k * 128 : k * 128 + 128
                    ]
        right = jnp.concatenate([scr_r[ss * 2], scr_r[ss * 2 + 1]], axis=1).astype(BF16)
        both = jnp.dot(leg_ref[ss], right, preferred_element_type=F32)
        base = jnp.maximum(first_ref[s], 0)
        x = jnp.where(row < 32 * JO, both[:ENTRIES, :128], both[:ENTRIES, 128:])
        y = jnp.where(degree >= base, both[ENTRIES:, 128:], both[ENTRIES:, :128])
        q = jnp.where(lane < 64, x, y)
        for jj in range(JR):
            scr_o[pl.ds(s * JR + jj, 32, stride=MROWS), :] = q[jj * 32 : jj * 32 + 32]

    @pl.when(group == NSG - 1)
    def _():
        out_ref[...] = scr_o[...].astype(BF16)


def run_legendre(first, incoming, table):
    return pl.pallas_call(
        legendre_kernel,
        grid_spec=pltpu.PrefetchScalarGridSpec(
            num_scalar_prefetch=1,
            grid=(NSG,),
            in_specs=[
                pl.BlockSpec((NLATD * 24, 2 * ROWS * CW), lambda g, f: (0, 0)),
                pl.BlockSpec((SG, 2 * ENTRIES, NLATD * ROWS), lambda g, f: (g, 0, 0)),
                pl.BlockSpec((512, 1024), lambda g, f: (0, 0)),
            ],
            out_specs=pl.BlockSpec((32 * MROWS, 128), lambda g, f: (0, 0)),
            scratch_shapes=[
                pltpu.VMEM((6, NLATD * 24, 128), F32),
                pltpu.VMEM((2 * SG, NLATD * ROWS, 128), F32),
                pltpu.VMEM((32 * MROWS, 128), F32),
            ],
        ),
        out_shape=jax.ShapeDtypeStruct((32 * MROWS, 128), BF16),
        compiler_params=pltpu.CompilerParams(vmem_limit_bytes=VMEM_LIMIT),
        name="legendre_forward",
    )(first, incoming, table, jnp.asarray(swap_mirror_table()))


def weights_kernel(w_ref, swap_ref, out_ref, scr):
    for zz in range(2):
        unpack_one(w_ref, swap_ref, out_ref, scr, zz)


def unpack_one(w_ref, swap_ref, out_ref, scr, zz):
    for h in range(2):
        for ih in range(2):
            t = [
                jnp.concatenate(
                    [
                        w_ref[zz, y * 8 + h * 4 + c, :, ih * 128 : ih * 128 + 128].astype(F32)
                        for y in range(NY)
                    ],
                    axis=0,
                )
                for c in range(4)
            ]
            for i4, u in enumerate(swap4(t, swap_ref[...])):
                for y in range(NY):
                    scr.at[zz * 2 + h][pl.ds(y * 8 + ih * 4 + i4, 2 * JO, stride=32), :] = u[
                        y * 2 * JO : (y + 1) * 2 * JO
                    ]
    for h in range(2):
        out_ref[:, :, zz, :, h * 128 : h * 128 + 128] = scr[zz * 2 + h].astype(BF16).reshape(2 * JO, NY, 8, 128)


def run_weights(gathered):
    return pl.pallas_call(
        weights_kernel,
        grid=(NZ // 2,),
        in_specs=[
            pl.BlockSpec((2, 32, 2 * JO, 256), lambda z: (z, 0, 0, 0)),
            pl.BlockSpec((512, 512), lambda z: (0, 0)),
        ],
        out_specs=pl.BlockSpec((2 * JO, NY, 2, 8, 256), lambda z: (0, 0, z, 0, 0)),
        scratch_shapes=[pltpu.VMEM((4, 2 * JO * 32, 128), F32)],
        out_shape=jax.ShapeDtypeStruct((2 * JO, NY, NZ, 8, 256), BF16),
        cost_estimate=pl.CostEstimate(flops=4 * 10**9, bytes_accessed=6 * 10**6, transcendentals=0),
        compiler_params=pltpu.CompilerParams(vmem_limit_bytes=VMEM_LIMIT),
        name="unpack_weights",
    )(gathered, jnp.asarray(swap_table()))


VROWS = NY * MROWS


def mix_kernel(owner_ref, d_ref, w_ref, a_ref, swap_ref, out_ref, v, ex):
    for y in range(NY):
        for h in range(2):
            t = [d_ref[y * 8 + h * 4 + i] for i in range(4)]
            for q, u in enumerate(swap4(t, swap_ref[...])):
                v[h, q * VROWS + y * MROWS : q * VROWS + (y + 1) * MROWS, :] = u
    v[:, 4 * VROWS :, :] = jnp.zeros((2, v.shape[1] - 4 * VROWS, 128), F32)
    lane_a = a_ref[...]

    def rows(q, jj):
        return jnp.concatenate(
            [
                jnp.concatenate(
                    [v.at[h][pl.ds(start, 16, stride=JR), :] for h in range(2)], axis=1
                )
                for start in (q * VROWS + y * MROWS + jj for y in range(NY))
            ],
            axis=0,
        )

    extra = jnp.concatenate([rows(0, JO), rows(1, JO)], axis=0).astype(BF16)
    ex[...] = jnp.zeros_like(ex)
    owner = owner_ref[0]

    def put(q, jj, value):
        for y in range(NY):
            start = q * VROWS + y * MROWS + jj
            for h in range(2):
                v.at[h][pl.ds(start, SLOTS, stride=JR), :] = value[
                    y * 16 : y * 16 + SLOTS, h * 128 : h * 128 + 128
                ]

    for jj in range(JO):
        j = owner * JO + jj
        x = jnp.concatenate([rows(0, jj), rows(1, jj)], axis=0).astype(BF16)
        yv = jnp.concatenate([rows(2, jj), rows(3, jj)], axis=0).astype(BF16)
        upper = jnp.dot(
            jnp.concatenate([x, yv, extra], axis=0), w_ref[JO + jj], preferred_element_type=F32
        )
        lower = jnp.dot(yv, w_ref[jj], preferred_element_type=F32)
        ym = jnp.where(lane_a <= j, lower, upper[128:256])
        ex[...] += jnp.where(lane_a == j, upper[256:384], 0.0)
        put(0, jj, upper[0:64])
        put(1, jj, upper[64:128])
        put(2, jj, ym[0:64])
        put(3, jj, ym[64:128])
    put(0, JO, ex[0:64, :])
    put(1, JO, ex[64:128, :])
    for y in range(NY):
        for h in range(2):
            t = [
                v[h, q * VROWS + y * MROWS : q * VROWS + (y + 1) * MROWS, :]
                for q in range(4)
            ]
            for i, u in enumerate(swap4(t, swap_ref[...])):
                out_ref[y * 8 + h * 4 + i] = u.astype(BF16)


def run_mix(owner, coeffs, weights, lower_orders):
    return pl.pallas_call(
        mix_kernel,
        in_specs=[
            pl.BlockSpec(memory_space=pltpu.SMEM),
            pl.BlockSpec(memory_space=pltpu.VMEM),
            pl.BlockSpec(memory_space=pltpu.VMEM),
            pl.BlockSpec(memory_space=pltpu.VMEM),
            pl.BlockSpec(memory_space=pltpu.VMEM),
        ],
        out_specs=pl.BlockSpec(memory_space=pltpu.VMEM),
        scratch_shapes=[pltpu.VMEM((2, 4 * VROWS + 64, 128), F32), pltpu.VMEM((128, 256), F32)],
        out_shape=jax.ShapeDtypeStruct((32, MROWS, 128), BF16),
        compiler_params=pltpu.CompilerParams(vmem_limit_bytes=VMEM_LIMIT),
        name="mix_degrees",
    )(owner, coeffs, weights, lower_orders, jnp.asarray(swap_table()))


def inverse_kernel(
    first_ref, d_ref, turned_ref, swap_ref, spec_ref, home_ref,
    scr_f, scr_b, scr_e, entries, leaving, send_sem, recv_sem, local_sem,
):
    group = pl.program_id(0)
    me = own_index("lat")
    barrier = pltpu.get_barrier_semaphore()

    @pl.when(group == 0)
    def _():
        greet("lat", NLATD, barrier)
        scr_f[...] = d_ref[...].astype(F32)

    row = lax.broadcasted_iota(jnp.int32, (ENTRIES, 128), 0)
    left = lax.broadcasted_iota(jnp.int32, (ENTRIES, 128), 1) < 64
    degree = JO * (row % 32) + row // 32
    for ss in range(SG):
        s = group * SG + ss
        q = jnp.concatenate(
            [scr_f[pl.ds(s * JR + jj, 32, stride=MROWS), :] for jj in range(JR)], axis=0
        )
        entries[s] = q.astype(BF16)
        qs = pltpu.roll(q, 64, 1)
        base = jnp.maximum(first_ref[s], 0)
        x = jnp.where(row < 32 * JO, jnp.where(left, q, 0.0), jnp.where(left, 0.0, qs)).astype(BF16)
        y = jnp.where(degree >= base, jnp.where(left, qs, 0.0), jnp.where(left, 0.0, q)).astype(BF16)
        scr_b[ss] = jnp.dot(turned_ref[ss, 0], x, preferred_element_type=F32) + jnp.dot(
            turned_ref[ss, 1], y, preferred_element_type=F32
        )
        t = [
            jnp.concatenate(
                [scr_b.at[ss][pl.ds(rg * 4 + r4, 32, stride=ROWS), :] for rg in range(3)], axis=0
            )
            for r4 in range(4)
        ]
        for qi, u in enumerate(swap4(t, swap_ref[...])):
            for rg in range(3):
                scr_e.at[(qi % 2) * 3 + rg][pl.ds((qi // 2) * SG + ss, 32, stride=EROWS), :] = u[
                    rg * 32 : rg * 32 + 32
                ]
    for k in range(6):
        leaving[group, :, :, k * 128 : k * 128 + 128] = (
            scr_e[k].reshape(NLATD, EROWS, 128).astype(BF16)
        )

    @pl.when(group == 0)
    def _():
        pl.semaphore_wait(barrier, NLATD - 1)

    def send(g, k):
        peer = peer_of("lat", k, 1)
        return pltpu.make_async_remote_copy(
            src_ref=leaving.at[g, peer],
            dst_ref=home_ref.at[g, me],
            send_sem=send_sem.at[g, k],
            recv_sem=recv_sem.at[g, k],
            device_id=partner("lat", peer),
            device_id_type=pl.DeviceIdType.MESH,
        )

    def start(k, carry):
        send(group, k).start()
        return carry

    lax.fori_loop(1, NLATD, start, 0)
    pltpu.make_async_copy(leaving.at[group, me], home_ref.at[group, me], local_sem.at[group]).start()

    @pl.when(group == NSG - 1)
    def _():
        def pack(s, carry):
            sx, sy = pair_one_hots(jnp.maximum(first_ref[s], 0))
            qt = jnp.transpose(entries[s].astype(F32)).astype(BF16)
            spec_ref[s] = (
                jnp.dot(qt[:64], sx, preferred_element_type=F32)
                + jnp.dot(qt[64:], sy, preferred_element_type=F32)
            ).astype(BF16)
            return carry

        lax.fori_loop(0, SLOTS, pack, 0)
        for g in range(NSG):

            def finish(k, carry):
                send(g, k).wait_send()
                source = peer_of("lat", k, -1)
                pltpu.make_async_remote_copy(
                    src_ref=leaving.at[g, source],
                    dst_ref=home_ref.at[g, source],
                    send_sem=send_sem.at[g, k],
                    recv_sem=recv_sem.at[g, k],
                    device_id=partner("lat", source),
                    device_id_type=pl.DeviceIdType.MESH,
                ).wait_recv()
                return carry

            lax.fori_loop(1, NLATD, finish, 0)
            pltpu.make_async_copy(leaving.at[g, me], home_ref.at[g, me], local_sem.at[g]).wait()


def run_inverse(first, mixed, turned):
    return pl.pallas_call(
        inverse_kernel,
        grid=(NSG,),
        in_specs=[
            pl.BlockSpec(memory_space=pltpu.SMEM),
            pl.BlockSpec((32 * MROWS, 128), lambda g: (0, 0)),
            pl.BlockSpec((SG, 2, NLATD * ROWS, ENTRIES), lambda g: (g, 0, 0, 0)),
            pl.BlockSpec((512, 512), lambda g: (0, 0)),
        ],
        out_specs=[
            pl.BlockSpec((SLOTS, 2 * CW, KP), lambda g: (0, 0, 0)),
            pl.BlockSpec(memory_space=pl.ANY),
        ],
        scratch_shapes=[
            pltpu.VMEM((32 * MROWS, 128), F32),
            pltpu.VMEM((SG, NLATD * ROWS, 128), F32),
            pltpu.VMEM((6, NLATD * EROWS, 128), F32),
            pltpu.VMEM((SLOTS, ENTRIES, 128), BF16),
            pltpu.VMEM((NSG, NLATD, EROWS, 2 * ROWS * CW), BF16),
            pltpu.SemaphoreType.DMA((NSG, NLATD)),
            pltpu.SemaphoreType.DMA((NSG, NLATD)),
            pltpu.SemaphoreType.DMA((NSG,)),
        ],
        out_shape=[
            jax.ShapeDtypeStruct((SLOTS, 2 * CW, KP), BF16),
            jax.ShapeDtypeStruct((NSG, NLATD, EROWS, 2 * ROWS * CW), BF16),
        ],
        compiler_params=pltpu.CompilerParams(
            vmem_limit_bytes=VMEM_LIMIT, collective_id=3, has_side_effects=True
        ),
        name="legendre_inverse_home",
    )(first, mixed, turned, jnp.asarray(swap_table()))


PIECES = ((0, 4, 0), (4, 6, 4), (6, 8, 0), (8, 12, 2))


def tail_kernel(
    x_ref, w_in_ref, w_out_ref, swap_ref, own_ref, left_ref, right_ref,
    recv, res, v, send_sem, recv_sem, local_sem, halo_send, halo_recv, own_sem,
):
    me = own_index("chan")
    band = own_index("lat")
    rightward = lax.rem(band + 1, NLATD)
    leftward = lax.rem(band + NLATD - 1, NLATD)
    barrier = pltpu.get_barrier_semaphore()
    greet("chan", NCH, barrier)
    for neighbour in (leftward, rightward):
        pl.semaphore_signal(
            barrier, inc=1, device_id=partner("lat", neighbour), device_id_type=pl.DeviceIdType.MESH
        )

    def local(rg):
        at = pl.ds(rg * 128, 128)
        return pltpu.make_async_copy(x_ref.at[me, :, at], recv.at[me, :, at], local_sem.at[rg])

    for rg in range(3):
        local(rg).start()
    pl.semaphore_wait(barrier, NCH + 1)

    def copy(rg, k, sign):
        peer = peer_of("chan", k, sign)
        at = pl.ds(rg * 128, 128)
        return pltpu.make_async_remote_copy(
            src_ref=x_ref.at[peer, :, at],
            dst_ref=recv.at[me if sign == 1 else peer, :, at],
            send_sem=send_sem.at[rg, k],
            recv_sem=recv_sem.at[rg, k],
            device_id=partner("chan", peer),
            device_id_type=pl.DeviceIdType.MESH,
        )

    for rg in range(3):

        def start(k, carry):
            copy(rg, k, 1).start()
            return carry

        lax.fori_loop(1, NCH, start, 0)

    def halo(piece):
        first, last, place = PIECES[piece]
        there = right_ref if piece < 2 else left_ref
        return pltpu.make_async_remote_copy(
            src_ref=res.at[pl.ds(first, last - first)],
            dst_ref=there.at[pl.ds(place, last - first)],
            send_sem=halo_send.at[piece],
            recv_sem=halo_recv.at[piece],
            device_id=partner("lat", leftward if piece < 2 else rightward),
            device_id_type=pl.DeviceIdType.MESH,
        )

    for rg in range(3):

        def arrive(k, carry):
            copy(rg, k, -1).wait_recv()
            return carry

        lax.fori_loop(1, NCH, arrive, 0)
        local(rg).wait()
        for h in range(2):
            t = [recv[h * 4 + i, :, rg * 128 : rg * 128 + 128] for i in range(4)]
            for r4, u in enumerate(swap4(t, swap_ref[...])):
                v[r4 * CHUNKP : (r4 + 1) * CHUNKP, h * 128 : h * 128 + 128] = u
        values = v[...]
        centered = values - jnp.mean(values, axis=-1, keepdims=True)
        normed = (
            centered * lax.rsqrt(jnp.mean(centered * centered, axis=-1, keepdims=True) + 1e-05)
        ).astype(BF16)
        hidden = jax.nn.gelu(
            jnp.dot(normed, w_in_ref[...], preferred_element_type=F32), approximate=True
        ).astype(BF16)
        result = (values + jnp.dot(hidden, w_out_ref[...], preferred_element_type=F32)).astype(BF16)
        for r4 in range(4):
            res[rg * 4 + r4] = result[r4 * CHUNKP : r4 * CHUNKP + CHUNK]
        for piece in ((0,), (1, 2), (3,))[rg]:
            halo(piece).start()
    own = pltpu.make_async_copy(res, own_ref, own_sem)
    own.start()
    for rg in range(3):

        def finish(k, carry):
            copy(rg, k, 1).wait_send()
            return carry

        lax.fori_loop(1, NCH, finish, 0)
    for piece in range(4):
        halo(piece).wait_send()
        halo(piece).wait_recv()
    own.wait()


def run_tail(state, w_in, w_out):
    return pl.pallas_call(
        tail_kernel,
        in_specs=[pl.BlockSpec(memory_space=pl.ANY)] + [pl.BlockSpec(memory_space=pltpu.VMEM)] * 3,
        out_specs=[pl.BlockSpec(memory_space=pl.ANY)] * 3,
        scratch_shapes=[
            pltpu.VMEM((NCH, CHUNKP, ROWS * CW), BF16),
            pltpu.VMEM((ROWS, CHUNK, 256), BF16),
            pltpu.VMEM((4 * CHUNKP, 256), F32),
            pltpu.SemaphoreType.DMA((3, NCH)),
            pltpu.SemaphoreType.DMA((3, NCH)),
            pltpu.SemaphoreType.DMA((3,)),
            pltpu.SemaphoreType.DMA((4,)),
            pltpu.SemaphoreType.DMA((4,)),
            pltpu.SemaphoreType.DMA,
        ],
        out_shape=[
            jax.ShapeDtypeStruct((ROWS, CHUNK, 256), BF16),
            jax.ShapeDtypeStruct((HALO, CHUNK, 256), BF16),
            jax.ShapeDtypeStruct((HALO, CHUNK, 256), BF16),
        ],
        compiler_params=pltpu.CompilerParams(
            vmem_limit_bytes=VMEM_LIMIT, collective_id=4, has_side_effects=True
        ),
        name="pointwise_tail",
    )(state, w_in, w_out, jnp.asarray(swap_table()))


def assemble_kernel(place_ref, left_ref, own_ref, right_ref, out_ref, scr):
    scr[...] = jnp.zeros_like(scr)
    for at, ref in ((0, left_ref), (HALO, own_ref), (HALO + ROWS, right_ref)):
        for k in range(ref.shape[0]):
            row = at + k + place_ref[0]

            @pl.when((row >= 0) & (row < place_ref[1]))
            def _():
                for h in range(2):
                    scr.at[h][pl.ds(row, CHUNK, stride=24), :] = ref[
                        k, :, h * 128 : h * 128 + 128
                    ].astype(F32)

    for h in range(2):
        out_ref[:, h * 128 : h * 128 + 128] = scr[h].astype(BF16)


def run_assemble(place, pieces):
    return pl.pallas_call(
        assemble_kernel,
        in_specs=[pl.BlockSpec(memory_space=pltpu.SMEM)] + [pl.BlockSpec(memory_space=pltpu.VMEM)] * 3,
        out_specs=pl.BlockSpec(memory_space=pltpu.VMEM),
        scratch_shapes=[pltpu.VMEM((2, CHUNK * 24, 128), F32)],
        out_shape=jax.ShapeDtypeStruct((CHUNK * 24, 256), BF16),
        compiler_params=pltpu.CompilerParams(vmem_limit_bytes=VMEM_LIMIT),
        name="assemble_bands",
    )(place, *pieces)


def partner(kind, index):
    y, z, c = lax.axis_index("y"), lax.axis_index("z"), lax.axis_index("chan")
    if kind == "lat":
        return (index // NZ, index % NZ, c)
    if kind == "own":
        return (index // NCH, z, index % NCH)
    return (y, z, index)


def own_index(kind):
    y, z, c = lax.axis_index("y"), lax.axis_index("z"), lax.axis_index("chan")
    if kind == "lat":
        return y * NZ + z
    if kind == "own":
        return y * NCH + c
    return c


def zigzag(j, n):
    half = (j + 1) // 2
    return jnp.where(j % 2 == 1, half, lax.rem(n - half, n))


def peer_of(kind, k, sign):
    me = own_index(kind)
    if kind == "chan":
        return lax.rem(me + sign * k + NCH, NCH)
    n = NLATD - k
    fast, slow = n // NY, n % NY
    y = lax.rem(me // 8 + sign * zigzag(slow, NY) + NY, NY)
    low = me % 8
    if kind == "lat":
        return y * 8 + lax.rem(low + sign * zigzag(fast, NZ) + NZ, NZ)
    x = lax.rem(low // 2 + sign * zigzag(fast // 2, 4) + 4, 4)
    return y * 8 + x * 2 + lax.rem(low % 2 + fast % 2, 2)


def greet(kind, n, barrier):
    me = own_index(kind)

    def one(k, carry):
        pl.semaphore_signal(
            barrier,
            inc=1,
            device_id=partner(kind, lax.rem(me + k, n)),
            device_id_type=pl.DeviceIdType.MESH,
        )
        return carry

    lax.fori_loop(1, n, one, 0)


def exchange_kernel(kind, n, x_ref, o_ref, send_sem, recv_sem, local_sem):
    me = own_index(kind)
    barrier = pltpu.get_barrier_semaphore()
    greet(kind, n, barrier)
    local = pltpu.make_async_copy(x_ref.at[me], o_ref.at[me], local_sem)
    local.start()
    pl.semaphore_wait(barrier, n - 1)

    def copy(k, sign):
        peer = peer_of(kind, k, sign)
        return pltpu.make_async_remote_copy(
            src_ref=x_ref.at[peer],
            dst_ref=o_ref.at[me if sign == 1 else peer],
            send_sem=send_sem.at[k],
            recv_sem=recv_sem.at[k],
            device_id=partner(kind, peer),
            device_id_type=pl.DeviceIdType.MESH,
        )

    def start(k, carry):
        copy(k, 1).start()
        return carry

    lax.fori_loop(1, n, start, 0)

    def finish(k, carry):
        copy(k, 1).wait_send()
        copy(k, -1).wait_recv()
        return carry

    lax.fori_loop(1, n, finish, 0)
    local.wait()


def outbound_kernel(
    x_ref, first_ref, leg_ref, o_ref, out_ref, turned_ref, send_sem, recv_sem, local_sem
):
    group = pl.program_id(0)
    me = own_index("lat")
    barrier = pltpu.get_barrier_semaphore()
    local = pltpu.make_async_copy(x_ref.at[me], o_ref.at[me], local_sem)

    def copy(k, sign):
        peer = peer_of("lat", k, sign)
        return pltpu.make_async_remote_copy(
            src_ref=x_ref.at[peer],
            dst_ref=o_ref.at[me if sign == 1 else peer],
            send_sem=send_sem.at[k],
            recv_sem=recv_sem.at[k],
            device_id=partner("lat", peer),
            device_id_type=pl.DeviceIdType.MESH,
        )

    @pl.when(group == 0)
    def _():
        greet("lat", NLATD, barrier)
        local.start()
        pl.semaphore_wait(barrier, NLATD - 1)

        def start(k, carry):
            copy(k, 1).start()
            return carry

        lax.fori_loop(1, NLATD, start, 0)

    for ss in range(SG):
        sx, sy = pair_one_hots(jnp.maximum(first_ref[group * SG + ss], 0))
        table = leg_ref[ss]
        x = jnp.dot(sx, table, preferred_element_type=F32)
        y = jnp.dot(sy, table, preferred_element_type=F32)
        out_ref[ss, :ENTRIES] = x.astype(BF16)
        out_ref[ss, ENTRIES:] = y.astype(BF16)
        turned_ref[ss, 0] = jnp.transpose(x).astype(BF16)
        turned_ref[ss, 1] = jnp.transpose(y).astype(BF16)

    @pl.when(group == NSG - 1)
    def _():
        def finish(k, carry):
            copy(k, 1).wait_send()
            copy(k, -1).wait_recv()
            return carry

        lax.fori_loop(1, NLATD, finish, 0)
        local.wait()


def run_outbound(spectra, first, legendre):
    return pl.pallas_call(
        outbound_kernel,
        grid=(NSG,),
        in_specs=[
            pl.BlockSpec(memory_space=pl.ANY),
            pl.BlockSpec(memory_space=pltpu.SMEM),
            pl.BlockSpec((SG, KP, NLATD * ROWS), lambda g: (g, 0, 0)),
        ],
        out_specs=[
            pl.BlockSpec(memory_space=pl.ANY),
            pl.BlockSpec((SG, 2 * ENTRIES, NLATD * ROWS), lambda g: (g, 0, 0)),
            pl.BlockSpec((SG, 2, NLATD * ROWS, ENTRIES), lambda g: (g, 0, 0, 0)),
        ],
        scratch_shapes=[
            pltpu.SemaphoreType.DMA((NLATD,)),
            pltpu.SemaphoreType.DMA((NLATD,)),
            pltpu.SemaphoreType.DMA,
        ],
        out_shape=[
            jax.ShapeDtypeStruct(spectra.shape, BF16),
            jax.ShapeDtypeStruct((SLOTS, 2 * ENTRIES, NLATD * ROWS), BF16),
            jax.ShapeDtypeStruct((SLOTS, 2, NLATD * ROWS, ENTRIES), BF16),
        ],
        compiler_params=pltpu.CompilerParams(
            vmem_limit_bytes=VMEM_LIMIT, collective_id=2, has_side_effects=True
        ),
        name="exchange_out_sort_table",
    )(spectra, first, legendre)


def opening_kernel(
    rows_ref, w_ref, left_ref, right_ref, o_ref, send_sem, recv_sem, local_sem, halo_send, halo_recv
):
    me = own_index("own")
    band = own_index("lat")
    rightward = lax.rem(band + 1, NLATD)
    leftward = lax.rem(band + NLATD - 1, NLATD)
    barrier = pltpu.get_barrier_semaphore()
    for neighbour in (leftward, rightward):
        pl.semaphore_signal(
            barrier, inc=1, device_id=partner("lat", neighbour), device_id_type=pl.DeviceIdType.MESH
        )
    greet("own", 32, barrier)
    local = pltpu.make_async_copy(w_ref.at[me], o_ref.at[me], local_sem)
    local.start()
    pl.semaphore_wait(barrier, 33)

    def halo(side):
        return pltpu.make_async_remote_copy(
            src_ref=rows_ref.at[pl.ds(side * (HALO + ROWS), HALO)],
            dst_ref=left_ref if side else right_ref,
            send_sem=halo_send.at[side],
            recv_sem=halo_recv.at[side],
            device_id=partner("lat", rightward if side else leftward),
            device_id_type=pl.DeviceIdType.MESH,
        )

    def copy(k, sign):
        peer = peer_of("own", k, sign)
        return pltpu.make_async_remote_copy(
            src_ref=w_ref.at[peer],
            dst_ref=o_ref.at[me if sign == 1 else peer],
            send_sem=send_sem.at[k],
            recv_sem=recv_sem.at[k],
            device_id=partner("own", peer),
            device_id_type=pl.DeviceIdType.MESH,
        )

    for side in range(2):
        halo(side).start()

    def start(k, carry):
        copy(k, 1).start()
        return carry

    lax.fori_loop(1, 32, start, 0)

    def finish(k, carry):
        copy(k, 1).wait_send()
        copy(k, -1).wait_recv()
        return carry

    lax.fori_loop(1, 32, finish, 0)
    local.wait()
    for side in range(2):
        halo(side).wait_send()
        halo(side).wait_recv()


def run_opening(rows, by_degree):
    return pl.pallas_call(
        opening_kernel,
        in_specs=[pl.BlockSpec(memory_space=pl.ANY)] * 2,
        out_specs=[pl.BlockSpec(memory_space=pl.ANY)] * 3,
        scratch_shapes=[
            pltpu.SemaphoreType.DMA((32,)),
            pltpu.SemaphoreType.DMA((32,)),
            pltpu.SemaphoreType.DMA,
            pltpu.SemaphoreType.DMA((2,)),
            pltpu.SemaphoreType.DMA((2,)),
        ],
        out_shape=[
            jax.ShapeDtypeStruct((HALO, CW, NLON), BF16),
            jax.ShapeDtypeStruct((HALO, CW, NLON), BF16),
            jax.ShapeDtypeStruct(by_degree.shape, BF16),
        ],
        compiler_params=pltpu.CompilerParams(collective_id=0, has_side_effects=True),
        name="opening_exchange",
    )(rows, by_degree)


def exchange(kind, collective, x):
    n = x.shape[0]
    return pl.pallas_call(
        functools.partial(exchange_kernel, kind, n),
        in_specs=[pl.BlockSpec(memory_space=pl.ANY)],
        out_specs=pl.BlockSpec(memory_space=pl.ANY),
        scratch_shapes=[
            pltpu.SemaphoreType.DMA((n,)),
            pltpu.SemaphoreType.DMA((n,)),
            pltpu.SemaphoreType.DMA,
        ],
        out_shape=jax.ShapeDtypeStruct(x.shape, x.dtype),
        compiler_params=pltpu.CompilerParams(collective_id=collective, has_side_effects=True),
        name="exchange_" + kind,
    )(x)


def order_columns(pairing):
    a = pairing.reshape(NLATD, 1, SLOTS)
    return jnp.where(a >= 0, jnp.concatenate([a, L - 1 - a], axis=1), -1)


def one_hot(col, width):
    return (col.reshape(-1)[:, None] == jnp.arange(width, dtype=jnp.int32)[None, :]).astype(BF16)


def dot_nt(a, b):
    return lax.dot_general(a, b, (((1,), (1,)), ((), ())), preferred_element_type=F32)


def per_device(grid_in, pairing, offsets, legendre, degree_mix, w_in, w_out):
    lat = ("y", "z")
    me = lax.axis_index("y") * NZ + lax.axis_index("z")
    chan = lax.axis_index("chan")
    start = jnp.take(offsets, me)
    length = jnp.take(offsets, me + 1) - start
    first = lax.dynamic_slice_in_dim(pairing, me * SLOTS, SLOTS)
    cap = grid_in.shape[0]

    rows = jnp.transpose(grid_in, (0, 2, 1))
    valid = (jnp.arange(cap, dtype=jnp.int32) < length)[:, None, None]
    rows = jnp.where(valid, rows, jnp.zeros((), BF16))
    shift = me * ROWS - HALO - start
    rows = jnp.concatenate([jnp.zeros((12, CW, NLON), BF16), rows], axis=0)
    virt = lax.dynamic_slice_in_dim(rows, 12 + shift, cap, axis=0)
    own = virt[HALO : HALO + ROWS]
    by_degree = dot_nt(
        jnp.asarray(degree_order()),
        jnp.transpose(degree_mix, (1, 2, 0)).reshape(8 * CW, L),
    ).astype(BF16)
    from_left, from_right, owned = run_opening(virt, by_degree.reshape(32, 2 * JO, 256))
    xt = (own + jnp.concatenate([from_left, from_right], axis=0)).reshape(ROWS * CW, NLON)
    gathered = lax.all_gather(owned, "z", axis=0, tiled=False)
    weights = run_weights(gathered)
    weights = weights.reshape(2 * JO, 256, 256)

    sides = order_columns(pairing)
    home = one_hot(sides.reshape(NLATD, 2, NSG, SG).transpose(2, 0, 1, 3), L)
    waves_back = inverse_table()
    inverse_re = dot_nt(jnp.asarray(waves_back[:, :L]), home).astype(BF16)
    inverse_im = dot_nt(jnp.asarray(waves_back[:, L:]), home).astype(BF16)
    padded = dot_nt(jnp.asarray(pad_rows()), xt).astype(BF16)

    waves = forward_table()
    by_order = lax.optimization_barrier(
        jnp.concatenate(
            [dot_nt(jnp.asarray(waves[:L]), xt).astype(BF16), dot_nt(jnp.asarray(waves[L:]), xt).astype(BF16)],
            axis=1,
        )
    )
    spectra = jnp.dot(one_hot(sides, L), by_order, preferred_element_type=F32).astype(BF16)
    incoming, table, turned = run_outbound(
        spectra.reshape(NLATD, 24, 2 * ROWS * CW), first, legendre
    )
    coeffs = run_legendre(first, incoming.reshape(NLATD * 24, 2 * ROWS * CW), table)
    at_owner = lax.all_to_all(
        coeffs.reshape(32, MROWS, 128), ("y", "chan"), split_axis=0, concat_axis=0, tiled=True
    )
    at_owner, weights, inverse_re, inverse_im, padded = lax.optimization_barrier(
        (at_owner, weights, inverse_re, inverse_im, padded)
    )
    owner = (lax.axis_index("y") * NCH + chan).reshape(1)
    z = lax.axis_index("z")
    a_here = lax.dynamic_slice_in_dim(pairing.reshape(NY, NZ, SLOTS), z, 1, axis=1)[:, 0]
    a_here = jnp.concatenate([a_here, jnp.full((NY, 4), -1, jnp.int32)], axis=1).reshape(1, NY * 16)
    a_here = jnp.broadcast_to(a_here, (2, NY * 16)).reshape(128, 1)
    mixed = run_mix(owner, at_owner, weights, a_here)
    returned = exchange("own", 1, mixed)
    spectrum, homeward = run_inverse(first, returned.reshape(32 * MROWS, 128), turned)
    spectrum = jnp.transpose(spectrum.reshape(SLOTS, 2, CW, KP), (0, 3, 1, 2))
    homeward = homeward.reshape(NLATD * 24, 2 * ROWS * CW)
    filtered = jnp.dot(
        inverse_re, homeward[:, : ROWS * CW], preferred_element_type=F32
    ) + jnp.dot(inverse_im, homeward[:, ROWS * CW :], preferred_element_type=F32)
    state = (padded.astype(F32) + filtered).astype(BF16)
    own_rows, out_left, out_right = run_tail(state.reshape(NCH, CHUNKP, ROWS * CW), w_in, w_out)
    place = jnp.stack([shift, length])
    grid_out = run_assemble(place, (out_left, own_rows, out_right))
    grid_out = jnp.transpose(grid_out.reshape(CHUNK, cap, 256), (1, 0, 2))
    return (grid_out, spectrum)


def solution(mesh):
    fine = Mesh(np.asarray(mesh.devices).reshape(NY, NZ, NCH), ("y", "z", "chan"))
    lat = ("y", "z")
    in_specs = (
        P(lat, None, "chan"),
        P(),
        P(),
        P(lat, None, None),
        P(None, lat, "chan"),
        P(),
        P(),
    )
    out_specs = (P(lat, "chan", None), P(lat, None, None, "chan"))
    return jax.shard_map(per_device, mesh=fine, in_specs=in_specs, out_specs=out_specs, check_vma=False)
```

```python
import functools
import math

import jax
import jax.numpy as jnp
import ml_dtypes
import numpy as np
from jax import lax
from jax.experimental import pallas as pl
from jax.experimental.pallas import tpu as pltpu
from jax.sharding import Mesh
from jax.sharding import PartitionSpec as P

NLON = 1440
L = 720
KP = 721
SLOTS = 12
ROWS = 12
HALO = 6
CW = 32
NCH = 8
NY = 4
NZ = 8
NLATD = 32
CHUNK = 180
CHUNKP = 192
NPADDED = NCH * CHUNKP
JO = 12
JR = JO + 1
ENTRIES = 32 * JR
MROWS = 160
SG = 4
NSG = SLOTS // SG
EROWS = 2 * SG
F32 = jnp.float32
BF16 = jnp.bfloat16
VMEM_LIMIT = 56 * 1024 * 1024


def forward_table():
    n = np.arange(NLON, dtype=np.int64)
    m = np.arange(L, dtype=np.int64)
    ph = ((m[:, None] * n[None, :]) % NLON).astype(np.float32) * np.float32(2.0 * math.pi / NLON)
    f = np.float32(1.0 / math.sqrt(NLON))
    table = np.concatenate([np.cos(ph) * f, -np.sin(ph) * f], axis=0)
    return table.astype(ml_dtypes.bfloat16)


def inverse_table():
    n = np.arange(NLON, dtype=np.int64)
    m = np.arange(L, dtype=np.int64)
    ph = ((n[:, None] * m[None, :]) % NLON).astype(np.float32) * np.float32(2.0 * math.pi / NLON)
    f = np.float32(1.0 / math.sqrt(NLON))
    w = np.where(m == 0, 1.0, 2.0).astype(np.float32)[None, :] * f
    table = np.concatenate([np.cos(ph) * w, -np.sin(ph) * w], axis=1)
    padded = np.zeros((NCH, CHUNKP, 2 * L), np.float32)
    padded[:, :CHUNK] = table.reshape(NCH, CHUNK, 2 * L)
    return padded.reshape(NPADDED, 2 * L).astype(ml_dtypes.bfloat16)


def pad_rows():
    sel = np.zeros((NCH, CHUNKP, NLON), np.float32)
    for c in range(NCH):
        for i in range(CHUNK):
            sel[c, i, c * CHUNK + i] = 1.0
    return sel.reshape(NPADDED, NLON).astype(ml_dtypes.bfloat16)


def degree_order():
    sel = np.zeros((32, 2 * JO, L), np.float32)
    for o in range(L // 2 // JO):
        for jj in range(JO):
            j = o * JO + jj
            sel[o, jj, j] = 1.0
            sel[o, JO + jj, L - 1 - j] = 1.0
    return sel.reshape(32 * 2 * JO, L).astype(ml_dtypes.bfloat16)


def swap_table():
    sel = np.zeros((4, 4, CW, 4, 4, CW), np.float32)
    for q in range(4):
        for r in range(4):
            for c in range(CW):
                sel[q, r, c, r, q, c] = 1.0
    return sel.reshape(512, 512).astype(ml_dtypes.bfloat16)


def swap_mirror_table():
    base = swap_table().reshape(512, 4, 4, CW)
    return np.concatenate([base, base[:, :, [2, 3, 0, 1]]], axis=2).reshape(512, 1024)


def swap4(v, table):
    joined = jnp.concatenate([x.astype(BF16) for x in v], axis=1)
    out = jnp.dot(joined, table, preferred_element_type=F32)
    width = out.shape[1] // 4
    return [out[:, k * width : (k + 1) * width] for k in range(4)]


def pair_one_hots(base):
    ri = lax.broadcasted_iota(jnp.int32, (32 * JR, 1), 0)
    jj = ri // 32
    o = ri % 32
    j = JO * o + jj
    regular = (jj < JO) & (j < L // 2)
    extra = (jj == JO) & (base // JO == o)
    kx = jnp.where(regular, L - 1 - base - j, jnp.where(extra, L - base, -1))
    ky = jnp.where(regular, jnp.where(j >= base, j - base, L - j), -1)
    col = lax.broadcasted_iota(jnp.int32, (32 * JR, KP), 1)
    sx = jnp.where(col == kx, 1.0, 0.0).astype(BF16)
    sy = jnp.where(col == ky, 1.0, 0.0).astype(BF16)
    return sx, sy


def legendre_slot(s, part, base, scr_f, table, swap, scr_r, scr_o):
    row = lax.broadcasted_iota(jnp.int32, (ENTRIES, 128), 0)
    lane = lax.broadcasted_iota(jnp.int32, (ENTRIES, 128), 1)
    degree = JO * (row % 32) + row // 32
    t = [
        jnp.concatenate(
            [scr_f.at[p * 3 + rg][pl.ds(side * SLOTS + s, 32, stride=24), :] for rg in range(3)], axis=0
        )
        for side in range(2)
        for p in range(2)
    ]
    for r4, u in enumerate(swap4(t, swap)):
        for rg in range(3):
            for k in range(2):
                scr_r.at[part * 2 + k][pl.ds(rg * 4 + r4, 32, stride=ROWS), :] = u[
                    rg * 32 : rg * 32 + 32, k * 128 : k * 128 + 128
                ]
    right = jnp.concatenate([scr_r[part * 2], scr_r[part * 2 + 1]], axis=1).astype(BF16)
    both = jnp.dot(table[s], right, preferred_element_type=F32)
    x = jnp.where(row < 32 * JO, both[:ENTRIES, :128], both[:ENTRIES, 128:])
    y = jnp.where(degree >= base, both[ENTRIES:, 128:], both[ENTRIES:, :128])
    q = jnp.where(lane < 64, x, y)
    for jj in range(JR):
        scr_o[pl.ds(s * JR + jj, 32, stride=MROWS), :] = q[jj * 32 : jj * 32 + 32]


def weights_kernel(w_ref, swap_ref, out_ref, scr):
    for zz in range(2):
        unpack_one(w_ref, swap_ref, out_ref, scr, zz)


def unpack_one(w_ref, swap_ref, out_ref, scr, zz):
    for h in range(2):
        for ih in range(2):
            t = [
                jnp.concatenate(
                    [
                        w_ref[zz, y * 8 + h * 4 + c, :, ih * 128 : ih * 128 + 128].astype(F32)
                        for y in range(NY)
                    ],
                    axis=0,
                )
                for c in range(4)
            ]
            for i4, u in enumerate(swap4(t, swap_ref[...])):
                for y in range(NY):
                    scr.at[zz * 2 + h][pl.ds(y * 8 + ih * 4 + i4, 2 * JO, stride=32), :] = u[
                        y * 2 * JO : (y + 1) * 2 * JO
                    ]
    for h in range(2):
        out_ref[:, :, zz, :, h * 128 : h * 128 + 128] = scr[zz * 2 + h].astype(BF16).reshape(2 * JO, NY, 8, 128)


def run_weights(gathered):
    return pl.pallas_call(
        weights_kernel,
        grid=(NZ // 2,),
        in_specs=[
            pl.BlockSpec((2, 32, 2 * JO, 256), lambda z: (z, 0, 0, 0)),
            pl.BlockSpec((512, 512), lambda z: (0, 0)),
        ],
        out_specs=pl.BlockSpec((2 * JO, NY, 2, 8, 256), lambda z: (0, 0, z, 0, 0)),
        scratch_shapes=[pltpu.VMEM((4, 2 * JO * 32, 128), F32)],
        out_shape=jax.ShapeDtypeStruct((2 * JO, NY, NZ, 8, 256), BF16),
        cost_estimate=pl.CostEstimate(flops=4 * 10**9, bytes_accessed=6 * 10**6, transcendentals=0),
        compiler_params=pltpu.CompilerParams(vmem_limit_bytes=VMEM_LIMIT),
        name="unpack_weights",
    )(gathered, jnp.asarray(swap_table()))


VROWS = NY * MROWS


def mix_kernel(
    owner_ref, d_ref, w_ref, a_ref, swap_ref, home_ref, v, ex, leaving, send_sem, recv_sem, local_sem
):
    me = own_index("own")
    barrier = pltpu.get_barrier_semaphore()
    greet("own", 32, barrier)
    for y in range(NY):
        for h in range(2):
            t = [d_ref[y * 8 + h * 4 + i] for i in range(4)]
            for q, u in enumerate(swap4(t, swap_ref[...])):
                v[h, q * VROWS + y * MROWS : q * VROWS + (y + 1) * MROWS, :] = u
    v[:, 4 * VROWS :, :] = jnp.zeros((2, v.shape[1] - 4 * VROWS, 128), F32)
    lane_a = a_ref[...]

    def rows(q, jj):
        return jnp.concatenate(
            [
                jnp.concatenate(
                    [v.at[h][pl.ds(start, 16, stride=JR), :] for h in range(2)], axis=1
                )
                for start in (q * VROWS + y * MROWS + jj for y in range(NY))
            ],
            axis=0,
        )

    extra = jnp.concatenate([rows(0, JO), rows(1, JO)], axis=0).astype(BF16)
    ex[...] = jnp.zeros_like(ex)
    owner = owner_ref[0]

    def put(q, jj, value):
        for y in range(NY):
            start = q * VROWS + y * MROWS + jj
            for h in range(2):
                v.at[h][pl.ds(start, SLOTS, stride=JR), :] = value[
                    y * 16 : y * 16 + SLOTS, h * 128 : h * 128 + 128
                ]

    for jj in range(JO):
        j = owner * JO + jj
        x = jnp.concatenate([rows(0, jj), rows(1, jj)], axis=0).astype(BF16)
        yv = jnp.concatenate([rows(2, jj), rows(3, jj)], axis=0).astype(BF16)
        upper = jnp.dot(
            jnp.concatenate([x, yv, extra], axis=0), w_ref[JO + jj], preferred_element_type=F32
        )
        lower = jnp.dot(yv, w_ref[jj], preferred_element_type=F32)
        ym = jnp.where(lane_a <= j, lower, upper[128:256])
        ex[...] += jnp.where(lane_a == j, upper[256:384], 0.0)
        put(0, jj, upper[0:64])
        put(1, jj, upper[64:128])
        put(2, jj, ym[0:64])
        put(3, jj, ym[64:128])
    put(0, JO, ex[0:64, :])
    put(1, JO, ex[64:128, :])
    for y in range(NY):
        for h in range(2):
            t = [
                v[h, q * VROWS + y * MROWS : q * VROWS + (y + 1) * MROWS, :]
                for q in range(4)
            ]
            for i, u in enumerate(swap4(t, swap_ref[...])):
                leaving[y * 8 + h * 4 + i] = u.astype(BF16)
    local = pltpu.make_async_copy(leaving.at[me], home_ref.at[me], local_sem)
    local.start()
    pl.semaphore_wait(barrier, 31)

    def copy(k, sign):
        peer = peer_of("own", k, sign)
        return pltpu.make_async_remote_copy(
            src_ref=leaving.at[peer],
            dst_ref=home_ref.at[me if sign == 1 else peer],
            send_sem=send_sem.at[k],
            recv_sem=recv_sem.at[k],
            device_id=partner("own", peer),
            device_id_type=pl.DeviceIdType.MESH,
        )

    def start(k, carry):
        copy(k, 1).start()
        return carry

    lax.fori_loop(1, 32, start, 0)

    def finish(k, carry):
        copy(k, 1).wait_send()
        copy(k, -1).wait_recv()
        return carry

    lax.fori_loop(1, 32, finish, 0)
    local.wait()


def run_mix(owner, coeffs, weights, lower_orders):
    return pl.pallas_call(
        mix_kernel,
        in_specs=[
            pl.BlockSpec(memory_space=pltpu.SMEM),
            pl.BlockSpec(memory_space=pltpu.VMEM),
            pl.BlockSpec(memory_space=pltpu.VMEM),
            pl.BlockSpec(memory_space=pltpu.VMEM),
            pl.BlockSpec(memory_space=pltpu.VMEM),
        ],
        out_specs=pl.BlockSpec(memory_space=pl.ANY),
        scratch_shapes=[pltpu.VMEM((2, 4 * VROWS + 64, 128), F32), pltpu.VMEM((128, 256), F32),
            pltpu.VMEM((32, MROWS, 128), BF16),
            pltpu.SemaphoreType.DMA((32,)),
            pltpu.SemaphoreType.DMA((32,)),
            pltpu.SemaphoreType.DMA,
        ],
        out_shape=jax.ShapeDtypeStruct((32, MROWS, 128), BF16),
        compiler_params=pltpu.CompilerParams(
            vmem_limit_bytes=VMEM_LIMIT, collective_id=1, has_side_effects=True
        ),
        name="mix_degrees",
    )(owner, coeffs, weights, lower_orders, jnp.asarray(swap_table()))


def inverse_kernel(
    first_ref, d_ref, turned_ref, swap_ref, spec_ref, home_ref,
    scr_f, scr_b, scr_e, entries, leaving, send_sem, recv_sem, local_sem,
):
    group = pl.program_id(0)
    me = own_index("lat")
    barrier = pltpu.get_barrier_semaphore()

    @pl.when(group == 0)
    def _():
        greet("lat", NLATD, barrier)
        scr_f[...] = d_ref[...].astype(F32)

    row = lax.broadcasted_iota(jnp.int32, (ENTRIES, 128), 0)
    left = lax.broadcasted_iota(jnp.int32, (ENTRIES, 128), 1) < 64
    degree = JO * (row % 32) + row // 32
    for ss in range(SG):
        s = group * SG + ss
        q = jnp.concatenate(
            [scr_f[pl.ds(s * JR + jj, 32, stride=MROWS), :] for jj in range(JR)], axis=0
        )
        entries[s] = q.astype(BF16)
        qs = pltpu.roll(q, 64, 1)
        base = jnp.maximum(first_ref[s], 0)
        x = jnp.where(row < 32 * JO, jnp.where(left, q, 0.0), jnp.where(left, 0.0, qs)).astype(BF16)
        y = jnp.where(degree >= base, jnp.where(left, qs, 0.0), jnp.where(left, 0.0, q)).astype(BF16)
        scr_b[ss] = jnp.dot(turned_ref[ss, 0], x, preferred_element_type=F32) + jnp.dot(
            turned_ref[ss, 1], y, preferred_element_type=F32
        )
        t = [
            jnp.concatenate(
                [scr_b.at[ss][pl.ds(rg * 4 + r4, 32, stride=ROWS), :] for rg in range(3)], axis=0
            )
            for r4 in range(4)
        ]
        for qi, u in enumerate(swap4(t, swap_ref[...])):
            for rg in range(3):
                scr_e.at[(qi % 2) * 3 + rg][pl.ds((qi // 2) * SG + ss, 32, stride=EROWS), :] = u[
                    rg * 32 : rg * 32 + 32
                ]
    for k in range(6):
        leaving[group, :, :, k * 128 : k * 128 + 128] = (
            scr_e[k].reshape(NLATD, EROWS, 128).astype(BF16)
        )

    @pl.when(group == 0)
    def _():
        pl.semaphore_wait(barrier, NLATD - 1)

    def send(g, k):
        peer = peer_of("lat", k, 1)
        return pltpu.make_async_remote_copy(
            src_ref=leaving.at[g, peer],
            dst_ref=home_ref.at[g, me],
            send_sem=send_sem.at[g, k],
            recv_sem=recv_sem.at[g, k],
            device_id=partner("lat", peer),
            device_id_type=pl.DeviceIdType.MESH,
        )

    def start(k, carry):
        send(group, k).start()
        return carry

    lax.fori_loop(1, NLATD, start, 0)
    pltpu.make_async_copy(leaving.at[group, me], home_ref.at[group, me], local_sem.at[group]).start()

    @pl.when(group == NSG - 1)
    def _():
        def pack(s, carry):
            sx, sy = pair_one_hots(jnp.maximum(first_ref[s], 0))
            qt = jnp.transpose(entries[s].astype(F32)).astype(BF16)
            spec_ref[s] = (
                jnp.dot(qt[:64], sx, preferred_element_type=F32)
                + jnp.dot(qt[64:], sy, preferred_element_type=F32)
            ).astype(BF16)
            return carry

        lax.fori_loop(0, SLOTS, pack, 0)
        for g in range(NSG):

            def finish(k, carry):
                send(g, k).wait_send()
                source = peer_of("lat", k, -1)
                pltpu.make_async_remote_copy(
                    src_ref=leaving.at[g, source],
                    dst_ref=home_ref.at[g, source],
                    send_sem=send_sem.at[g, k],
                    recv_sem=recv_sem.at[g, k],
                    device_id=partner("lat", source),
                    device_id_type=pl.DeviceIdType.MESH,
                ).wait_recv()
                return carry

            lax.fori_loop(1, NLATD, finish, 0)
            pltpu.make_async_copy(leaving.at[g, me], home_ref.at[g, me], local_sem.at[g]).wait()


def run_inverse(first, mixed, turned):
    return pl.pallas_call(
        inverse_kernel,
        grid=(NSG,),
        in_specs=[
            pl.BlockSpec(memory_space=pltpu.SMEM),
            pl.BlockSpec((32 * MROWS, 128), lambda g: (0, 0)),
            pl.BlockSpec((SG, 2, NLATD * ROWS, ENTRIES), lambda g: (g, 0, 0, 0)),
            pl.BlockSpec((512, 512), lambda g: (0, 0)),
        ],
        out_specs=[
            pl.BlockSpec((SLOTS, 2 * CW, KP), lambda g: (0, 0, 0)),
            pl.BlockSpec(memory_space=pl.ANY),
        ],
        scratch_shapes=[
            pltpu.VMEM((32 * MROWS, 128), F32),
            pltpu.VMEM((SG, NLATD * ROWS, 128), F32),
            pltpu.VMEM((6, NLATD * EROWS, 128), F32),
            pltpu.VMEM((SLOTS, ENTRIES, 128), BF16),
            pltpu.VMEM((NSG, NLATD, EROWS, 2 * ROWS * CW), BF16),
            pltpu.SemaphoreType.DMA((NSG, NLATD)),
            pltpu.SemaphoreType.DMA((NSG, NLATD)),
            pltpu.SemaphoreType.DMA((NSG,)),
        ],
        out_shape=[
            jax.ShapeDtypeStruct((SLOTS, 2 * CW, KP), BF16),
            jax.ShapeDtypeStruct((NSG, NLATD, EROWS, 2 * ROWS * CW), BF16),
        ],
        compiler_params=pltpu.CompilerParams(
            vmem_limit_bytes=VMEM_LIMIT, collective_id=3, has_side_effects=True
        ),
        name="legendre_inverse_home",
    )(first, mixed, turned, jnp.asarray(swap_table()))


GROUP_ORDER = (0, 2, 1)
PIECES = ((0, 4, 0), (4, 6, 4), (6, 8, 0), (8, 12, 2))


def tail_kernel(
    x_ref, w_in_ref, w_out_ref, swap_ref, own_ref, left_ref, right_ref,
    recv, res, v, send_sem, recv_sem, local_sem, halo_send, halo_recv, own_sem,
):
    me = own_index("chan")
    band = own_index("lat")
    rightward = lax.rem(band + 1, NLATD)
    leftward = lax.rem(band + NLATD - 1, NLATD)
    barrier = pltpu.get_barrier_semaphore()
    greet("chan", NCH, barrier)
    for neighbour in (leftward, rightward):
        pl.semaphore_signal(
            barrier, inc=1, device_id=partner("lat", neighbour), device_id_type=pl.DeviceIdType.MESH
        )

    def local(rg):
        at = pl.ds(rg * 128, 128)
        return pltpu.make_async_copy(x_ref.at[me, :, at], recv.at[me, :, at], local_sem.at[rg])

    for rg in range(3):
        local(rg).start()
    pl.semaphore_wait(barrier, NCH + 1)

    def copy(rg, k, sign):
        peer = peer_of("chan", k, sign)
        at = pl.ds(rg * 128, 128)
        return pltpu.make_async_remote_copy(
            src_ref=x_ref.at[peer, :, at],
            dst_ref=recv.at[me if sign == 1 else peer, :, at],
            send_sem=send_sem.at[rg, k],
            recv_sem=recv_sem.at[rg, k],
            device_id=partner("chan", peer),
            device_id_type=pl.DeviceIdType.MESH,
        )

    def start_group(rg):
        def start(k, carry):
            copy(rg, k, 1).start()
            return carry

        lax.fori_loop(1, NCH, start, 0)

    def group_left(rg):
        def finish(k, carry):
            copy(rg, k, 1).wait_send()
            return carry

        lax.fori_loop(1, NCH, finish, 0)

    start_group(GROUP_ORDER[0])

    def halo(piece):
        first, last, place = PIECES[piece]
        there = right_ref if piece < 2 else left_ref
        return pltpu.make_async_remote_copy(
            src_ref=res.at[pl.ds(first, last - first)],
            dst_ref=there.at[pl.ds(place, last - first)],
            send_sem=halo_send.at[piece],
            recv_sem=halo_recv.at[piece],
            device_id=partner("lat", leftward if piece < 2 else rightward),
            device_id_type=pl.DeviceIdType.MESH,
        )

    for place, rg in enumerate(GROUP_ORDER):
        group_left(rg)
        if place < 2:
            start_group(GROUP_ORDER[place + 1])

        def arrive(k, carry):
            copy(rg, k, -1).wait_recv()
            return carry

        lax.fori_loop(1, NCH, arrive, 0)
        local(rg).wait()
        for h in range(2):
            t = [recv[h * 4 + i, :, rg * 128 : rg * 128 + 128] for i in range(4)]
            for r4, u in enumerate(swap4(t, swap_ref[...])):
                v[r4 * CHUNKP : (r4 + 1) * CHUNKP, h * 128 : h * 128 + 128] = u
        values = v[...]
        centered = values - jnp.mean(values, axis=-1, keepdims=True)
        normed = (
            centered * lax.rsqrt(jnp.mean(centered * centered, axis=-1, keepdims=True) + 1e-05)
        ).astype(BF16)
        hidden = jax.nn.gelu(
            jnp.dot(normed, w_in_ref[...], preferred_element_type=F32), approximate=True
        ).astype(BF16)
        result = (values + jnp.dot(hidden, w_out_ref[...], preferred_element_type=F32)).astype(BF16)
        for r4 in range(4):
            res[rg * 4 + r4] = result[r4 * CHUNKP : r4 * CHUNKP + CHUNK]
        for piece in ((0,), (1, 2), (3,))[rg]:
            halo(piece).start()
    own = pltpu.make_async_copy(res, own_ref, own_sem)
    own.start()
    for piece in range(4):
        halo(piece).wait_send()
        halo(piece).wait_recv()
    own.wait()


def run_tail(state, w_in, w_out):
    return pl.pallas_call(
        tail_kernel,
        in_specs=[pl.BlockSpec(memory_space=pl.ANY)] + [pl.BlockSpec(memory_space=pltpu.VMEM)] * 3,
        out_specs=[pl.BlockSpec(memory_space=pl.ANY)] * 3,
        scratch_shapes=[
            pltpu.VMEM((NCH, CHUNKP, ROWS * CW), BF16),
            pltpu.VMEM((ROWS, CHUNK, 256), BF16),
            pltpu.VMEM((4 * CHUNKP, 256), F32),
            pltpu.SemaphoreType.DMA((3, NCH)),
            pltpu.SemaphoreType.DMA((3, NCH)),
            pltpu.SemaphoreType.DMA((3,)),
            pltpu.SemaphoreType.DMA((4,)),
            pltpu.SemaphoreType.DMA((4,)),
            pltpu.SemaphoreType.DMA,
        ],
        out_shape=[
            jax.ShapeDtypeStruct((ROWS, CHUNK, 256), BF16),
            jax.ShapeDtypeStruct((HALO, CHUNK, 256), BF16),
            jax.ShapeDtypeStruct((HALO, CHUNK, 256), BF16),
        ],
        compiler_params=pltpu.CompilerParams(
            vmem_limit_bytes=VMEM_LIMIT, collective_id=4, has_side_effects=True
        ),
        name="pointwise_tail",
    )(state, w_in, w_out, jnp.asarray(swap_table()))


def assemble_kernel(place_ref, left_ref, own_ref, right_ref, out_ref, scr):
    scr[...] = jnp.zeros_like(scr)
    for at, ref in ((0, left_ref), (HALO, own_ref), (HALO + ROWS, right_ref)):
        for k in range(ref.shape[0]):
            row = at + k + place_ref[0]

            @pl.when((row >= 0) & (row < place_ref[1]))
            def _():
                for h in range(2):
                    scr.at[h][pl.ds(row, CHUNK, stride=24), :] = ref[
                        k, :, h * 128 : h * 128 + 128
                    ].astype(F32)

    for h in range(2):
        out_ref[:, h * 128 : h * 128 + 128] = scr[h].astype(BF16)


def run_assemble(place, pieces):
    return pl.pallas_call(
        assemble_kernel,
        in_specs=[pl.BlockSpec(memory_space=pltpu.SMEM)] + [pl.BlockSpec(memory_space=pltpu.VMEM)] * 3,
        out_specs=pl.BlockSpec(memory_space=pltpu.VMEM),
        scratch_shapes=[pltpu.VMEM((2, CHUNK * 24, 128), F32)],
        out_shape=jax.ShapeDtypeStruct((CHUNK * 24, 256), BF16),
        compiler_params=pltpu.CompilerParams(vmem_limit_bytes=VMEM_LIMIT),
        name="assemble_bands",
    )(place, *pieces)


def partner(kind, index):
    y, z, c = lax.axis_index("y"), lax.axis_index("z"), lax.axis_index("chan")
    if kind == "lat":
        return (index // NZ, index % NZ, c)
    if kind == "own":
        return (index // NCH, z, index % NCH)
    return (y, z, index)


def own_index(kind):
    y, z, c = lax.axis_index("y"), lax.axis_index("z"), lax.axis_index("chan")
    if kind == "lat":
        return y * NZ + z
    if kind == "own":
        return y * NCH + c
    return c


def zigzag(j, n):
    half = (j + 1) // 2
    return jnp.where(j % 2 == 1, half, lax.rem(n - half, n))


def peer_of(kind, k, sign):
    me = own_index(kind)
    if kind == "chan":
        return lax.rem(me + sign * k + NCH, NCH)
    n = NLATD - k
    fast, slow = n // NY, n % NY
    y = lax.rem(me // 8 + sign * zigzag(slow, NY) + NY, NY)
    low = me % 8
    if kind == "lat":
        return y * 8 + lax.rem(low + sign * zigzag(fast, NZ) + NZ, NZ)
    x = lax.rem(low // 2 + sign * zigzag(fast // 2, 4) + 4, 4)
    return y * 8 + x * 2 + lax.rem(low % 2 + fast % 2, 2)


def greet(kind, n, barrier):
    me = own_index(kind)

    def one(k, carry):
        pl.semaphore_signal(
            barrier,
            inc=1,
            device_id=partner(kind, lax.rem(me + k, n)),
            device_id_type=pl.DeviceIdType.MESH,
        )
        return carry

    lax.fori_loop(1, n, one, 0)


def outbound_kernel(
    x_ref, first_ref, leg_ref, swap_ref, coeff_ref, turned_ref,
    arrived, table, scr_f, scr_r, scr_o, send_sem, recv_sem, local_sem,
):
    group = pl.program_id(0)
    me = own_index("lat")
    barrier = pltpu.get_barrier_semaphore()
    local = pltpu.make_async_copy(x_ref.at[me], arrived.at[me], local_sem)

    def copy(k, sign):
        peer = peer_of("lat", k, sign)
        return pltpu.make_async_remote_copy(
            src_ref=x_ref.at[peer],
            dst_ref=arrived.at[me if sign == 1 else peer],
            send_sem=send_sem.at[k],
            recv_sem=recv_sem.at[k],
            device_id=partner("lat", peer),
            device_id_type=pl.DeviceIdType.MESH,
        )

    @pl.when(group == 0)
    def _():
        greet("lat", NLATD, barrier)
        local.start()
        pl.semaphore_wait(barrier, NLATD - 1)

        def start(k, carry):
            copy(k, 1).start()
            return carry

        lax.fori_loop(1, NLATD, start, 0)

    for ss in range(SG):
        sx, sy = pair_one_hots(jnp.maximum(first_ref[group * SG + ss], 0))
        packed = leg_ref[ss]
        x = jnp.dot(sx, packed, preferred_element_type=F32)
        y = jnp.dot(sy, packed, preferred_element_type=F32)
        table[group * SG + ss, :ENTRIES] = x.astype(BF16)
        table[group * SG + ss, ENTRIES:] = y.astype(BF16)
        turned_ref[ss, 0] = jnp.transpose(x).astype(BF16)
        turned_ref[ss, 1] = jnp.transpose(y).astype(BF16)

    @pl.when(group == NSG - 1)
    def _():
        def finish(k, carry):
            copy(k, 1).wait_send()
            copy(k, -1).wait_recv()
            return carry

        lax.fori_loop(1, NLATD, finish, 0)
        local.wait()
        for k in range(6):
            scr_f[k] = (
                arrived[:, :, k * 128 : k * 128 + 128].astype(F32).reshape(NLATD * 2 * SLOTS, 128)
            )
        scr_o[...] = jnp.zeros_like(scr_o)

        def four(g, carry):
            for ss in range(SG):
                s = g * SG + ss
                base = jnp.maximum(first_ref[s], 0)
                legendre_slot(s, ss, base, scr_f, table, swap_ref[...], scr_r, scr_o)
            return carry

        lax.fori_loop(0, NSG, four, 0)
        coeff_ref[...] = scr_o[...].astype(BF16)


def run_outbound(spectra, first, legendre):
    return pl.pallas_call(
        outbound_kernel,
        grid=(NSG,),
        in_specs=[
            pl.BlockSpec(memory_space=pl.ANY),
            pl.BlockSpec(memory_space=pltpu.SMEM),
            pl.BlockSpec((SG, KP, NLATD * ROWS), lambda g: (g, 0, 0)),
            pl.BlockSpec((512, 1024), lambda g: (0, 0)),
        ],
        out_specs=[
            pl.BlockSpec((32 * MROWS, 128), lambda g: (0, 0)),
            pl.BlockSpec((SG, 2, NLATD * ROWS, ENTRIES), lambda g: (g, 0, 0, 0)),
        ],
        scratch_shapes=[
            pltpu.VMEM((NLATD, 2 * SLOTS, 2 * ROWS * CW), BF16),
            pltpu.VMEM((SLOTS, 2 * ENTRIES, NLATD * ROWS), BF16),
            pltpu.VMEM((6, NLATD * 24, 128), F32),
            pltpu.VMEM((2 * SG, NLATD * ROWS, 128), F32),
            pltpu.VMEM((32 * MROWS, 128), F32),
            pltpu.SemaphoreType.DMA((NLATD,)),
            pltpu.SemaphoreType.DMA((NLATD,)),
            pltpu.SemaphoreType.DMA,
        ],
        out_shape=[
            jax.ShapeDtypeStruct((32 * MROWS, 128), BF16),
            jax.ShapeDtypeStruct((SLOTS, 2, NLATD * ROWS, ENTRIES), BF16),
        ],
        compiler_params=pltpu.CompilerParams(
            vmem_limit_bytes=VMEM_LIMIT, collective_id=2, has_side_effects=True
        ),
        name="outbound_legendre",
    )(spectra, first, legendre, jnp.asarray(swap_mirror_table()))


def opening_kernel(
    rows_ref, w_ref, left_ref, right_ref, o_ref, send_sem, recv_sem, local_sem, halo_send, halo_recv
):
    me = own_index("own")
    band = own_index("lat")
    rightward = lax.rem(band + 1, NLATD)
    leftward = lax.rem(band + NLATD - 1, NLATD)
    barrier = pltpu.get_barrier_semaphore()
    for neighbour in (leftward, rightward):
        pl.semaphore_signal(
            barrier, inc=1, device_id=partner("lat", neighbour), device_id_type=pl.DeviceIdType.MESH
        )
    greet("own", 32, barrier)
    local = pltpu.make_async_copy(w_ref.at[me], o_ref.at[me], local_sem)
    local.start()
    pl.semaphore_wait(barrier, 33)

    def halo(side, row):
        return pltpu.make_async_remote_copy(
            src_ref=rows_ref.at[side * (HALO + ROWS) + row],
            dst_ref=(left_ref if side else right_ref).at[row],
            send_sem=halo_send.at[side, row],
            recv_sem=halo_recv.at[side, row],
            device_id=partner("lat", rightward if side else leftward),
            device_id_type=pl.DeviceIdType.MESH,
        )

    def copy(k, sign):
        peer = peer_of("own", k, sign)
        return pltpu.make_async_remote_copy(
            src_ref=w_ref.at[peer],
            dst_ref=o_ref.at[me if sign == 1 else peer],
            send_sem=send_sem.at[k],
            recv_sem=recv_sem.at[k],
            device_id=partner("own", peer),
            device_id_type=pl.DeviceIdType.MESH,
        )

    for row in range(HALO):
        for side in range(2):
            halo(side, row).start()

    def start(k, carry):
        copy(k, 1).start()
        return carry

    lax.fori_loop(1, 32, start, 0)

    def finish(k, carry):
        copy(k, 1).wait_send()
        copy(k, -1).wait_recv()
        return carry

    lax.fori_loop(1, 32, finish, 0)
    local.wait()
    for side in range(2):
        for row in range(HALO):
            halo(side, row).wait_send()
            halo(side, row).wait_recv()


def run_opening(rows, by_degree):
    return pl.pallas_call(
        opening_kernel,
        in_specs=[pl.BlockSpec(memory_space=pl.ANY)] * 2,
        out_specs=[pl.BlockSpec(memory_space=pl.ANY)] * 3,
        scratch_shapes=[
            pltpu.SemaphoreType.DMA((32,)),
            pltpu.SemaphoreType.DMA((32,)),
            pltpu.SemaphoreType.DMA,
            pltpu.SemaphoreType.DMA((2, HALO)),
            pltpu.SemaphoreType.DMA((2, HALO)),
        ],
        out_shape=[
            jax.ShapeDtypeStruct((HALO, CW, NLON), BF16),
            jax.ShapeDtypeStruct((HALO, CW, NLON), BF16),
            jax.ShapeDtypeStruct(by_degree.shape, BF16),
        ],
        compiler_params=pltpu.CompilerParams(collective_id=0, has_side_effects=True),
        name="opening_exchange",
    )(rows, by_degree)


def order_columns(pairing):
    a = pairing.reshape(NLATD, 1, SLOTS)
    return jnp.where(a >= 0, jnp.concatenate([a, L - 1 - a], axis=1), -1)


def one_hot(col, width):
    return (col.reshape(-1)[:, None] == jnp.arange(width, dtype=jnp.int32)[None, :]).astype(BF16)


def dot_nt(a, b):
    return lax.dot_general(a, b, (((1,), (1,)), ((), ())), preferred_element_type=F32)


def per_device(grid_in, pairing, offsets, legendre, degree_mix, w_in, w_out):
    lat = ("y", "z")
    me = lax.axis_index("y") * NZ + lax.axis_index("z")
    chan = lax.axis_index("chan")
    start = jnp.take(offsets, me)
    length = jnp.take(offsets, me + 1) - start
    first = lax.dynamic_slice_in_dim(pairing, me * SLOTS, SLOTS)
    cap = grid_in.shape[0]

    rows = jnp.transpose(grid_in, (0, 2, 1))
    valid = (jnp.arange(cap, dtype=jnp.int32) < length)[:, None, None]
    rows = jnp.where(valid, rows, jnp.zeros((), BF16))
    shift = me * ROWS - HALO - start
    rows = jnp.concatenate([jnp.zeros((12, CW, NLON), BF16), rows], axis=0)
    virt = lax.dynamic_slice_in_dim(rows, 12 + shift, cap, axis=0)
    own = virt[HALO : HALO + ROWS]
    by_degree = dot_nt(
        jnp.asarray(degree_order()),
        jnp.transpose(degree_mix, (1, 2, 0)).reshape(8 * CW, L),
    ).astype(BF16)
    from_left, from_right, owned = run_opening(virt, by_degree.reshape(32, 2 * JO, 256))
    xt = (own + jnp.concatenate([from_left, from_right], axis=0)).reshape(ROWS * CW, NLON)
    gathered = lax.all_gather(owned, "z", axis=0, tiled=False)
    weights = run_weights(gathered)
    weights = weights.reshape(2 * JO, 256, 256)

    sides = order_columns(pairing)
    home = one_hot(sides.reshape(NLATD, 2, NSG, SG).transpose(2, 0, 1, 3), L)
    waves_back = inverse_table()
    inverse_re = dot_nt(jnp.asarray(waves_back[:, :L]), home).astype(BF16)
    inverse_im = dot_nt(jnp.asarray(waves_back[:, L:]), home).astype(BF16)
    padded = dot_nt(jnp.asarray(pad_rows()), xt).astype(BF16)

    waves = forward_table()
    by_order = lax.optimization_barrier(
        jnp.concatenate(
            [dot_nt(jnp.asarray(waves[:L]), xt).astype(BF16), dot_nt(jnp.asarray(waves[L:]), xt).astype(BF16)],
            axis=1,
        )
    )
    spectra = jnp.dot(one_hot(sides, L), by_order, preferred_element_type=F32).astype(BF16)
    coeffs, turned = run_outbound(spectra.reshape(NLATD, 24, 2 * ROWS * CW), first, legendre)
    at_owner = lax.all_to_all(
        coeffs.reshape(32, MROWS, 128), ("y", "chan"), split_axis=0, concat_axis=0, tiled=True
    )
    at_owner, weights, inverse_re, inverse_im, padded = lax.optimization_barrier(
        (at_owner, weights, inverse_re, inverse_im, padded)
    )
    owner = (lax.axis_index("y") * NCH + chan).reshape(1)
    z = lax.axis_index("z")
    a_here = lax.dynamic_slice_in_dim(pairing.reshape(NY, NZ, SLOTS), z, 1, axis=1)[:, 0]
    a_here = jnp.concatenate([a_here, jnp.full((NY, 4), -1, jnp.int32)], axis=1).reshape(1, NY * 16)
    a_here = jnp.broadcast_to(a_here, (2, NY * 16)).reshape(128, 1)
    mixed = run_mix(owner, at_owner, weights, a_here)
    spectrum, homeward = run_inverse(first, mixed.reshape(32 * MROWS, 128), turned)
    spectrum = jnp.transpose(spectrum.reshape(SLOTS, 2, CW, KP), (0, 3, 1, 2))
    homeward = homeward.reshape(NLATD * 24, 2 * ROWS * CW)
    filtered = jnp.dot(
        inverse_re, homeward[:, : ROWS * CW], preferred_element_type=F32
    ) + jnp.dot(inverse_im, homeward[:, ROWS * CW :], preferred_element_type=F32)
    state = (padded.astype(F32) + filtered).astype(BF16)
    own_rows, out_left, out_right = run_tail(state.reshape(NCH, CHUNKP, ROWS * CW), w_in, w_out)
    place = jnp.stack([shift, length])
    grid_out = run_assemble(place, (out_left, own_rows, out_right))
    grid_out = jnp.transpose(grid_out.reshape(CHUNK, cap, 256), (1, 0, 2))
    return (grid_out, spectrum)


def solution(mesh):
    fine = Mesh(np.asarray(mesh.devices).reshape(NY, NZ, NCH), ("y", "z", "chan"))
    lat = ("y", "z")
    in_specs = (
        P(lat, None, "chan"),
        P(),
        P(),
        P(lat, None, None),
        P(None, lat, "chan"),
        P(),
        P(),
    )
    out_specs = (P(lat, "chan", None), P(lat, None, None, "chan"))
    return jax.shard_map(per_device, mesh=fine, in_specs=in_specs, out_specs=out_specs, check_vma=False)
```

```python
import functools
import math

import jax
import jax.numpy as jnp
import ml_dtypes
import numpy as np
from jax import lax
from jax.experimental import pallas as pl
from jax.experimental.pallas import tpu as pltpu
from jax.sharding import Mesh
from jax.sharding import PartitionSpec as P

NLON = 1440
L = 720
KP = 721
SLOTS = 12
ROWS = 12
HALO = 6
CW = 32
NCH = 8
NY = 4
NZ = 8
NLATD = 32
CHUNK = 180
CHUNKP = 192
NPADDED = NCH * CHUNKP
JO = 12
JR = JO + 1
ENTRIES = 32 * JR
MROWS = 160
SG = 4
NSG = SLOTS // SG
EROWS = 2 * SG
F32 = jnp.float32
BF16 = jnp.bfloat16
VMEM_LIMIT = 56 * 1024 * 1024


def forward_table():
    n = np.arange(NLON, dtype=np.int64)
    m = np.arange(L, dtype=np.int64)
    ph = ((m[:, None] * n[None, :]) % NLON).astype(np.float32) * np.float32(2.0 * math.pi / NLON)
    f = np.float32(1.0 / math.sqrt(NLON))
    table = np.concatenate([np.cos(ph) * f, -np.sin(ph) * f], axis=0)
    return table.astype(ml_dtypes.bfloat16)


def inverse_table():
    n = np.arange(NLON, dtype=np.int64)
    m = np.arange(L, dtype=np.int64)
    ph = ((n[:, None] * m[None, :]) % NLON).astype(np.float32) * np.float32(2.0 * math.pi / NLON)
    f = np.float32(1.0 / math.sqrt(NLON))
    w = np.where(m == 0, 1.0, 2.0).astype(np.float32)[None, :] * f
    table = np.concatenate([np.cos(ph) * w, -np.sin(ph) * w], axis=1)
    padded = np.zeros((NCH, CHUNKP, 2 * L), np.float32)
    padded[:, :CHUNK] = table.reshape(NCH, CHUNK, 2 * L)
    return padded.reshape(NPADDED, 2 * L).astype(ml_dtypes.bfloat16)


def pad_rows():
    sel = np.zeros((NCH, CHUNKP, NLON), np.float32)
    for c in range(NCH):
        for i in range(CHUNK):
            sel[c, i, c * CHUNK + i] = 1.0
    return sel.reshape(NPADDED, NLON).astype(ml_dtypes.bfloat16)


def degree_order():
    sel = np.zeros((32, 2 * JO, L), np.float32)
    for o in range(L // 2 // JO):
        for jj in range(JO):
            j = o * JO + jj
            sel[o, jj, j] = 1.0
            sel[o, JO + jj, L - 1 - j] = 1.0
    return sel.reshape(32 * 2 * JO, L).astype(ml_dtypes.bfloat16)


def swap_table():
    sel = np.zeros((4, 4, CW, 4, 4, CW), np.float32)
    for q in range(4):
        for r in range(4):
            for c in range(CW):
                sel[q, r, c, r, q, c] = 1.0
    return sel.reshape(512, 512).astype(ml_dtypes.bfloat16)


def swap_mirror_table():
    base = swap_table().reshape(512, 4, 4, CW)
    return np.concatenate([base, base[:, :, [2, 3, 0, 1]]], axis=2).reshape(512, 1024)


def swap4(v, table):
    joined = jnp.concatenate([x.astype(BF16) for x in v], axis=1)
    out = jnp.dot(joined, table, preferred_element_type=F32)
    width = out.shape[1] // 4
    return [out[:, k * width : (k + 1) * width] for k in range(4)]


def pair_one_hots(base):
    ri = lax.broadcasted_iota(jnp.int32, (32 * JR, 1), 0)
    jj = ri // 32
    o = ri % 32
    j = JO * o + jj
    regular = (jj < JO) & (j < L // 2)
    extra = (jj == JO) & (base // JO == o)
    kx = jnp.where(regular, L - 1 - base - j, jnp.where(extra, L - base, -1))
    ky = jnp.where(regular, jnp.where(j >= base, j - base, L - j), -1)
    col = lax.broadcasted_iota(jnp.int32, (32 * JR, KP), 1)
    sx = jnp.where(col == kx, 1.0, 0.0).astype(BF16)
    sy = jnp.where(col == ky, 1.0, 0.0).astype(BF16)
    return sx, sy


def legendre_slot(s, part, base, scr_f, table, swap, scr_r, scr_o):
    row = lax.broadcasted_iota(jnp.int32, (ENTRIES, 128), 0)
    lane = lax.broadcasted_iota(jnp.int32, (ENTRIES, 128), 1)
    degree = JO * (row % 32) + row // 32
    t = [
        jnp.concatenate(
            [scr_f.at[p * 3 + rg][pl.ds(side * SLOTS + s, 32, stride=24), :] for rg in range(3)], axis=0
        )
        for side in range(2)
        for p in range(2)
    ]
    for r4, u in enumerate(swap4(t, swap)):
        for rg in range(3):
            for k in range(2):
                scr_r.at[part * 2 + k][pl.ds(rg * 4 + r4, 32, stride=ROWS), :] = u[
                    rg * 32 : rg * 32 + 32, k * 128 : k * 128 + 128
                ]
    right = jnp.concatenate([scr_r[part * 2], scr_r[part * 2 + 1]], axis=1).astype(BF16)
    both = jnp.dot(table[s], right, preferred_element_type=F32)
    x = jnp.where(row < 32 * JO, both[:ENTRIES, :128], both[:ENTRIES, 128:])
    y = jnp.where(degree >= base, both[ENTRIES:, 128:], both[ENTRIES:, :128])
    q = jnp.where(lane < 64, x, y)
    for jj in range(JR):
        scr_o[pl.ds(s * JR + jj, 32, stride=MROWS), :] = q[jj * 32 : jj * 32 + 32]


def weights_kernel(w_ref, swap_ref, out_ref, scr):
    for zz in range(2):
        unpack_one(w_ref, swap_ref, out_ref, scr, zz)


def unpack_one(w_ref, swap_ref, out_ref, scr, zz):
    for h in range(2):
        for ih in range(2):
            t = [
                jnp.concatenate(
                    [
                        w_ref[zz, y * 8 + h * 4 + c, :, ih * 128 : ih * 128 + 128].astype(F32)
                        for y in range(NY)
                    ],
                    axis=0,
                )
                for c in range(4)
            ]
            for i4, u in enumerate(swap4(t, swap_ref[...])):
                for y in range(NY):
                    scr.at[zz * 2 + h][pl.ds(y * 8 + ih * 4 + i4, 2 * JO, stride=32), :] = u[
                        y * 2 * JO : (y + 1) * 2 * JO
                    ]
    for h in range(2):
        out_ref[:, :, zz, :, h * 128 : h * 128 + 128] = scr[zz * 2 + h].astype(BF16).reshape(2 * JO, NY, 8, 128)


def run_weights(gathered):
    return pl.pallas_call(
        weights_kernel,
        grid=(NZ // 2,),
        in_specs=[
            pl.BlockSpec((2, 32, 2 * JO, 256), lambda z: (z, 0, 0, 0)),
            pl.BlockSpec((512, 512), lambda z: (0, 0)),
        ],
        out_specs=pl.BlockSpec((2 * JO, NY, 2, 8, 256), lambda z: (0, 0, z, 0, 0)),
        scratch_shapes=[pltpu.VMEM((4, 2 * JO * 32, 128), F32)],
        out_shape=jax.ShapeDtypeStruct((2 * JO, NY, NZ, 8, 256), BF16),
        cost_estimate=pl.CostEstimate(flops=4 * 10**9, bytes_accessed=6 * 10**6, transcendentals=0),
        compiler_params=pltpu.CompilerParams(vmem_limit_bytes=VMEM_LIMIT),
        name="unpack_weights",
    )(gathered, jnp.asarray(swap_table()))


VROWS = NY * MROWS


def mix_kernel(
    owner_ref, d_ref, w_ref, a_ref, swap_ref, home_ref, v, ex, leaving, send_sem, recv_sem, local_sem
):
    me = own_index("own")
    barrier = pltpu.get_barrier_semaphore()
    greet("own", 32, barrier)
    for y in range(NY):
        for h in range(2):
            t = [d_ref[y * 8 + h * 4 + i] for i in range(4)]
            for q, u in enumerate(swap4(t, swap_ref[...])):
                v[h, q * VROWS + y * MROWS : q * VROWS + (y + 1) * MROWS, :] = u
    v[:, 4 * VROWS :, :] = jnp.zeros((2, v.shape[1] - 4 * VROWS, 128), F32)
    lane_a = a_ref[...]

    def rows(q, jj):
        return jnp.concatenate(
            [
                jnp.concatenate(
                    [v.at[h][pl.ds(start, 16, stride=JR), :] for h in range(2)], axis=1
                )
                for start in (q * VROWS + y * MROWS + jj for y in range(NY))
            ],
            axis=0,
        )

    extra = jnp.concatenate([rows(0, JO), rows(1, JO)], axis=0).astype(BF16)
    ex[...] = jnp.zeros_like(ex)
    owner = owner_ref[0]

    def put(q, jj, value):
        for y in range(NY):
            start = q * VROWS + y * MROWS + jj
            for h in range(2):
                v.at[h][pl.ds(start, SLOTS, stride=JR), :] = value[
                    y * 16 : y * 16 + SLOTS, h * 128 : h * 128 + 128
                ]

    for jj in range(JO):
        j = owner * JO + jj
        x = jnp.concatenate([rows(0, jj), rows(1, jj)], axis=0).astype(BF16)
        yv = jnp.concatenate([rows(2, jj), rows(3, jj)], axis=0).astype(BF16)
        upper = jnp.dot(
            jnp.concatenate([x, yv, extra], axis=0), w_ref[JO + jj], preferred_element_type=F32
        )
        lower = jnp.dot(yv, w_ref[jj], preferred_element_type=F32)
        ym = jnp.where(lane_a <= j, lower, upper[128:256])
        ex[...] += jnp.where(lane_a == j, upper[256:384], 0.0)
        put(0, jj, upper[0:64])
        put(1, jj, upper[64:128])
        put(2, jj, ym[0:64])
        put(3, jj, ym[64:128])
    put(0, JO, ex[0:64, :])
    put(1, JO, ex[64:128, :])
    for y in range(NY):
        for h in range(2):
            t = [
                v[h, q * VROWS + y * MROWS : q * VROWS + (y + 1) * MROWS, :]
                for q in range(4)
            ]
            for i, u in enumerate(swap4(t, swap_ref[...])):
                leaving[y * 8 + h * 4 + i] = u.astype(BF16)
    local = pltpu.make_async_copy(leaving.at[me], home_ref.at[me], local_sem)
    local.start()
    pl.semaphore_wait(barrier, 31)

    def copy(k, sign):
        peer = peer_of("own", k, sign)
        return pltpu.make_async_remote_copy(
            src_ref=leaving.at[peer],
            dst_ref=home_ref.at[me if sign == 1 else peer],
            send_sem=send_sem.at[k],
            recv_sem=recv_sem.at[k],
            device_id=partner("own", peer),
            device_id_type=pl.DeviceIdType.MESH,
        )

    def start(k, carry):
        copy(k, 1).start()
        return carry

    lax.fori_loop(1, 32, start, 0)

    def finish(k, carry):
        copy(k, 1).wait_send()
        copy(k, -1).wait_recv()
        return carry

    lax.fori_loop(1, 32, finish, 0)
    local.wait()


def run_mix(owner, coeffs, weights, lower_orders):
    return pl.pallas_call(
        mix_kernel,
        in_specs=[
            pl.BlockSpec(memory_space=pltpu.SMEM),
            pl.BlockSpec(memory_space=pltpu.VMEM),
            pl.BlockSpec(memory_space=pltpu.VMEM),
            pl.BlockSpec(memory_space=pltpu.VMEM),
            pl.BlockSpec(memory_space=pltpu.VMEM),
        ],
        out_specs=pl.BlockSpec(memory_space=pl.ANY),
        scratch_shapes=[pltpu.VMEM((2, 4 * VROWS + 64, 128), F32), pltpu.VMEM((128, 256), F32),
            pltpu.VMEM((32, MROWS, 128), BF16),
            pltpu.SemaphoreType.DMA((32,)),
            pltpu.SemaphoreType.DMA((32,)),
            pltpu.SemaphoreType.DMA,
        ],
        out_shape=jax.ShapeDtypeStruct((32, MROWS, 128), BF16),
        compiler_params=pltpu.CompilerParams(
            vmem_limit_bytes=VMEM_LIMIT, collective_id=1, has_side_effects=True
        ),
        name="mix_degrees",
    )(owner, coeffs, weights, lower_orders, jnp.asarray(swap_table()))


def inverse_kernel(
    first_ref, d_ref, turned_ref, swap_ref, spec_ref, home_ref,
    scr_f, scr_b, scr_e, entries, leaving, send_sem, recv_sem, local_sem,
):
    group = pl.program_id(0)
    me = own_index("lat")
    barrier = pltpu.get_barrier_semaphore()

    @pl.when(group == 0)
    def _():
        greet("lat", NLATD, barrier)
        scr_f[...] = d_ref[...].astype(F32)

    row = lax.broadcasted_iota(jnp.int32, (ENTRIES, 128), 0)
    left = lax.broadcasted_iota(jnp.int32, (ENTRIES, 128), 1) < 64
    degree = JO * (row % 32) + row // 32
    for ss in range(SG):
        s = group * SG + ss
        q = jnp.concatenate(
            [scr_f[pl.ds(s * JR + jj, 32, stride=MROWS), :] for jj in range(JR)], axis=0
        )
        entries[s] = q.astype(BF16)
        qs = pltpu.roll(q, 64, 1)
        base = jnp.maximum(first_ref[s], 0)
        x = jnp.where(row < 32 * JO, jnp.where(left, q, 0.0), jnp.where(left, 0.0, qs)).astype(BF16)
        y = jnp.where(degree >= base, jnp.where(left, qs, 0.0), jnp.where(left, 0.0, q)).astype(BF16)
        scr_b[ss] = jnp.dot(turned_ref[ss, 0], x, preferred_element_type=F32) + jnp.dot(
            turned_ref[ss, 1], y, preferred_element_type=F32
        )
        t = [
            jnp.concatenate(
                [scr_b.at[ss][pl.ds(rg * 4 + r4, 32, stride=ROWS), :] for rg in range(3)], axis=0
            )
            for r4 in range(4)
        ]
        for qi, u in enumerate(swap4(t, swap_ref[...])):
            for rg in range(3):
                scr_e.at[(qi % 2) * 3 + rg][pl.ds((qi // 2) * SG + ss, 32, stride=EROWS), :] = u[
                    rg * 32 : rg * 32 + 32
                ]
    for k in range(6):
        leaving[group, :, :, k * 128 : k * 128 + 128] = (
            scr_e[k].reshape(NLATD, EROWS, 128).astype(BF16)
        )

    @pl.when(group == 0)
    def _():
        pl.semaphore_wait(barrier, NLATD - 1)

    def send(g, k):
        peer = peer_of("lat", k, 1)
        return pltpu.make_async_remote_copy(
            src_ref=leaving.at[g, peer],
            dst_ref=home_ref.at[g, me],
            send_sem=send_sem.at[g, k],
            recv_sem=recv_sem.at[g, k],
            device_id=partner("lat", peer),
            device_id_type=pl.DeviceIdType.MESH,
        )

    def start(k, carry):
        send(group, k).start()
        return carry

    lax.fori_loop(1, NLATD, start, 0)
    pltpu.make_async_copy(leaving.at[group, me], home_ref.at[group, me], local_sem.at[group]).start()

    @pl.when(group == NSG - 1)
    def _():
        def pack(s, carry):
            sx, sy = pair_one_hots(jnp.maximum(first_ref[s], 0))
            qt = jnp.transpose(entries[s].astype(F32)).astype(BF16)
            spec_ref[s] = (
                jnp.dot(qt[:64], sx, preferred_element_type=F32)
                + jnp.dot(qt[64:], sy, preferred_element_type=F32)
            ).astype(BF16)
            return carry

        lax.fori_loop(0, SLOTS, pack, 0)
        for g in range(NSG):

            def finish(k, carry):
                send(g, k).wait_send()
                source = peer_of("lat", k, -1)
                pltpu.make_async_remote_copy(
                    src_ref=leaving.at[g, source],
                    dst_ref=home_ref.at[g, source],
                    send_sem=send_sem.at[g, k],
                    recv_sem=recv_sem.at[g, k],
                    device_id=partner("lat", source),
                    device_id_type=pl.DeviceIdType.MESH,
                ).wait_recv()
                return carry

            lax.fori_loop(1, NLATD, finish, 0)
            pltpu.make_async_copy(leaving.at[g, me], home_ref.at[g, me], local_sem.at[g]).wait()


def run_inverse(first, mixed, turned):
    return pl.pallas_call(
        inverse_kernel,
        grid=(NSG,),
        in_specs=[
            pl.BlockSpec(memory_space=pltpu.SMEM),
            pl.BlockSpec((32 * MROWS, 128), lambda g: (0, 0)),
            pl.BlockSpec((SG, 2, NLATD * ROWS, ENTRIES), lambda g: (g, 0, 0, 0)),
            pl.BlockSpec((512, 512), lambda g: (0, 0)),
        ],
        out_specs=[
            pl.BlockSpec((SLOTS, 2 * CW, KP), lambda g: (0, 0, 0)),
            pl.BlockSpec(memory_space=pl.ANY),
        ],
        scratch_shapes=[
            pltpu.VMEM((32 * MROWS, 128), F32),
            pltpu.VMEM((SG, NLATD * ROWS, 128), F32),
            pltpu.VMEM((6, NLATD * EROWS, 128), F32),
            pltpu.VMEM((SLOTS, ENTRIES, 128), BF16),
            pltpu.VMEM((NSG, NLATD, EROWS, 2 * ROWS * CW), BF16),
            pltpu.SemaphoreType.DMA((NSG, NLATD)),
            pltpu.SemaphoreType.DMA((NSG, NLATD)),
            pltpu.SemaphoreType.DMA((NSG,)),
        ],
        out_shape=[
            jax.ShapeDtypeStruct((SLOTS, 2 * CW, KP), BF16),
            jax.ShapeDtypeStruct((NSG, NLATD, EROWS, 2 * ROWS * CW), BF16),
        ],
        compiler_params=pltpu.CompilerParams(
            vmem_limit_bytes=VMEM_LIMIT, collective_id=3, has_side_effects=True
        ),
        name="legendre_inverse_home",
    )(first, mixed, turned, jnp.asarray(swap_table()))


GROUP_ORDER = (0, 2, 1)
PIECES = ((0, 4, 0), (4, 6, 4), (6, 8, 0), (8, 12, 2))


def tail_kernel(
    x_ref, w_in_ref, w_out_ref, swap_ref, own_ref, left_ref, right_ref,
    recv, res, v, send_sem, recv_sem, local_sem, halo_send, halo_recv, own_sem,
):
    me = own_index("chan")
    band = own_index("lat")
    rightward = lax.rem(band + 1, NLATD)
    leftward = lax.rem(band + NLATD - 1, NLATD)
    barrier = pltpu.get_barrier_semaphore()
    greet("chan", NCH, barrier)
    for neighbour in (leftward, rightward):
        pl.semaphore_signal(
            barrier, inc=1, device_id=partner("lat", neighbour), device_id_type=pl.DeviceIdType.MESH
        )

    def local(rg):
        at = pl.ds(rg * 128, 128)
        return pltpu.make_async_copy(x_ref.at[me, :, at], recv.at[me, :, at], local_sem.at[rg])

    for rg in range(3):
        local(rg).start()
    pl.semaphore_wait(barrier, NCH + 1)

    def copy(rg, k, sign):
        peer = peer_of("chan", k, sign)
        at = pl.ds(rg * 128, 128)
        return pltpu.make_async_remote_copy(
            src_ref=x_ref.at[peer, :, at],
            dst_ref=recv.at[me if sign == 1 else peer, :, at],
            send_sem=send_sem.at[rg, k],
            recv_sem=recv_sem.at[rg, k],
            device_id=partner("chan", peer),
            device_id_type=pl.DeviceIdType.MESH,
        )

    def start_group(rg):
        def start(k, carry):
            copy(rg, k, 1).start()
            return carry

        lax.fori_loop(1, NCH, start, 0)

    def group_left(rg):
        def finish(k, carry):
            copy(rg, k, 1).wait_send()
            return carry

        lax.fori_loop(1, NCH, finish, 0)

    start_group(GROUP_ORDER[0])

    def halo(piece):
        first, last, place = PIECES[piece]
        there = right_ref if piece < 2 else left_ref
        return pltpu.make_async_remote_copy(
            src_ref=res.at[pl.ds(first, last - first)],
            dst_ref=there.at[pl.ds(place, last - first)],
            send_sem=halo_send.at[piece],
            recv_sem=halo_recv.at[piece],
            device_id=partner("lat", leftward if piece < 2 else rightward),
            device_id_type=pl.DeviceIdType.MESH,
        )

    for place, rg in enumerate(GROUP_ORDER):
        group_left(rg)
        if place < 2:
            start_group(GROUP_ORDER[place + 1])

        def arrive(k, carry):
            copy(rg, k, -1).wait_recv()
            return carry

        lax.fori_loop(1, NCH, arrive, 0)
        local(rg).wait()
        for h in range(2):
            t = [recv[h * 4 + i, :, rg * 128 : rg * 128 + 128] for i in range(4)]
            for r4, u in enumerate(swap4(t, swap_ref[...])):
                v[r4 * CHUNKP : (r4 + 1) * CHUNKP, h * 128 : h * 128 + 128] = u
        values = v[...]
        centered = values - jnp.mean(values, axis=-1, keepdims=True)
        normed = (
            centered * lax.rsqrt(jnp.mean(centered * centered, axis=-1, keepdims=True) + 1e-05)
        ).astype(BF16)
        hidden = jax.nn.gelu(
            jnp.dot(normed, w_in_ref[...], preferred_element_type=F32), approximate=True
        ).astype(BF16)
        result = (values + jnp.dot(hidden, w_out_ref[...], preferred_element_type=F32)).astype(BF16)
        for r4 in range(4):
            res[rg * 4 + r4] = result[r4 * CHUNKP : r4 * CHUNKP + CHUNK]
        for piece in ((0,), (1, 2), (3,))[rg]:
            halo(piece).start()
    own = pltpu.make_async_copy(res, own_ref, own_sem)
    own.start()
    for piece in range(4):
        halo(piece).wait_send()
        halo(piece).wait_recv()
    own.wait()


def run_tail(state, w_in, w_out):
    return pl.pallas_call(
        tail_kernel,
        in_specs=[pl.BlockSpec(memory_space=pl.ANY)] + [pl.BlockSpec(memory_space=pltpu.VMEM)] * 3,
        out_specs=[pl.BlockSpec(memory_space=pl.ANY)] * 3,
        scratch_shapes=[
            pltpu.VMEM((NCH, CHUNKP, ROWS * CW), BF16),
            pltpu.VMEM((ROWS, CHUNK, 256), BF16),
            pltpu.VMEM((4 * CHUNKP, 256), F32),
            pltpu.SemaphoreType.DMA((3, NCH)),
            pltpu.SemaphoreType.DMA((3, NCH)),
            pltpu.SemaphoreType.DMA((3,)),
            pltpu.SemaphoreType.DMA((4,)),
            pltpu.SemaphoreType.DMA((4,)),
            pltpu.SemaphoreType.DMA,
        ],
        out_shape=[
            jax.ShapeDtypeStruct((ROWS, CHUNK, 256), BF16),
            jax.ShapeDtypeStruct((HALO, CHUNK, 256), BF16),
            jax.ShapeDtypeStruct((HALO, CHUNK, 256), BF16),
        ],
        compiler_params=pltpu.CompilerParams(
            vmem_limit_bytes=VMEM_LIMIT, collective_id=4, has_side_effects=True
        ),
        name="pointwise_tail",
    )(state, w_in, w_out, jnp.asarray(swap_table()))


def assemble_kernel(place_ref, left_ref, own_ref, right_ref, out_ref, scr):
    scr[...] = jnp.zeros_like(scr)
    for at, ref in ((0, left_ref), (HALO, own_ref), (HALO + ROWS, right_ref)):
        for k in range(ref.shape[0]):
            row = at + k + place_ref[0]

            @pl.when((row >= 0) & (row < place_ref[1]))
            def _():
                for h in range(2):
                    scr.at[h][pl.ds(row, CHUNK, stride=24), :] = ref[
                        k, :, h * 128 : h * 128 + 128
                    ].astype(F32)

    for h in range(2):
        out_ref[:, h * 128 : h * 128 + 128] = scr[h].astype(BF16)


def run_assemble(place, pieces):
    return pl.pallas_call(
        assemble_kernel,
        in_specs=[pl.BlockSpec(memory_space=pltpu.SMEM)] + [pl.BlockSpec(memory_space=pltpu.VMEM)] * 3,
        out_specs=pl.BlockSpec(memory_space=pltpu.VMEM),
        scratch_shapes=[pltpu.VMEM((2, CHUNK * 24, 128), F32)],
        out_shape=jax.ShapeDtypeStruct((CHUNK * 24, 256), BF16),
        compiler_params=pltpu.CompilerParams(vmem_limit_bytes=VMEM_LIMIT),
        name="assemble_bands",
    )(place, *pieces)


def partner(kind, index):
    y, z, c = lax.axis_index("y"), lax.axis_index("z"), lax.axis_index("chan")
    if kind == "lat":
        return (index // NZ, index % NZ, c)
    if kind == "own":
        return (index // NCH, z, index % NCH)
    return (y, z, index)


def own_index(kind):
    y, z, c = lax.axis_index("y"), lax.axis_index("z"), lax.axis_index("chan")
    if kind == "lat":
        return y * NZ + z
    if kind == "own":
        return y * NCH + c
    return c


def zigzag(j, n):
    half = (j + 1) // 2
    return jnp.where(j % 2 == 1, half, lax.rem(n - half, n))


def peer_of(kind, k, sign):
    me = own_index(kind)
    if kind == "chan":
        return lax.rem(me + sign * k + NCH, NCH)
    n = NLATD - k
    fast, slow = n // NY, n % NY
    y = lax.rem(me // 8 + sign * zigzag(slow, NY) + NY, NY)
    low = me % 8
    if kind == "lat":
        return y * 8 + lax.rem(low + sign * zigzag(fast, NZ) + NZ, NZ)
    x = lax.rem(low // 2 + sign * zigzag(fast // 2, 4) + 4, 4)
    return y * 8 + x * 2 + lax.rem(low % 2 + fast % 2, 2)


def greet(kind, n, barrier):
    me = own_index(kind)

    def one(k, carry):
        pl.semaphore_signal(
            barrier,
            inc=1,
            device_id=partner(kind, lax.rem(me + k, n)),
            device_id_type=pl.DeviceIdType.MESH,
        )
        return carry

    lax.fori_loop(1, n, one, 0)


def outbound_kernel(
    x_ref, first_ref, leg_ref, swap_ref, wave_re_ref, wave_im_ref, home_ref,
    coeff_ref, turned_ref, inverse_re_ref, inverse_im_ref,
    arrived, table, scr_f, scr_r, scr_o, send_sem, recv_sem, local_sem,
):
    group = pl.program_id(0)
    me = own_index("lat")
    barrier = pltpu.get_barrier_semaphore()
    local = pltpu.make_async_copy(x_ref.at[me], arrived.at[me], local_sem)

    def copy(k, sign):
        peer = peer_of("lat", k, sign)
        return pltpu.make_async_remote_copy(
            src_ref=x_ref.at[peer],
            dst_ref=arrived.at[me if sign == 1 else peer],
            send_sem=send_sem.at[k],
            recv_sem=recv_sem.at[k],
            device_id=partner("lat", peer),
            device_id_type=pl.DeviceIdType.MESH,
        )

    @pl.when(group == 0)
    def _():
        greet("lat", NLATD, barrier)
        local.start()
        pl.semaphore_wait(barrier, NLATD - 1)

        def start(k, carry):
            copy(k, 1).start()
            return carry

        lax.fori_loop(1, NLATD, start, 0)

    for ss in range(SG):
        sx, sy = pair_one_hots(jnp.maximum(first_ref[group * SG + ss], 0))
        packed = leg_ref[ss]
        x = jnp.dot(sx, packed, preferred_element_type=F32)
        y = jnp.dot(sy, packed, preferred_element_type=F32)
        table[group * SG + ss, :ENTRIES] = x.astype(BF16)
        table[group * SG + ss, ENTRIES:] = y.astype(BF16)
        turned_ref[ss, 0] = jnp.transpose(x).astype(BF16)
        turned_ref[ss, 1] = jnp.transpose(y).astype(BF16)
    inverse_re_ref[...] = jnp.dot(
        wave_re_ref[...], home_ref[...], preferred_element_type=F32
    ).astype(BF16)
    inverse_im_ref[...] = jnp.dot(
        wave_im_ref[...], home_ref[...], preferred_element_type=F32
    ).astype(BF16)

    @pl.when(group == NSG - 1)
    def _():
        def finish(k, carry):
            copy(k, 1).wait_send()
            copy(k, -1).wait_recv()
            return carry

        lax.fori_loop(1, NLATD, finish, 0)
        local.wait()
        for k in range(6):
            scr_f[k] = (
                arrived[:, :, k * 128 : k * 128 + 128].astype(F32).reshape(NLATD * 2 * SLOTS, 128)
            )
        scr_o[...] = jnp.zeros_like(scr_o)

        def four(g, carry):
            for ss in range(SG):
                s = g * SG + ss
                base = jnp.maximum(first_ref[s], 0)
                legendre_slot(s, ss, base, scr_f, table, swap_ref[...], scr_r, scr_o)
            return carry

        lax.fori_loop(0, NSG, four, 0)
        coeff_ref[...] = scr_o[...].astype(BF16)


def run_outbound(spectra, first, legendre, home):
    waves = inverse_table()
    return pl.pallas_call(
        outbound_kernel,
        grid=(NSG,),
        in_specs=[
            pl.BlockSpec(memory_space=pl.ANY),
            pl.BlockSpec(memory_space=pltpu.SMEM),
            pl.BlockSpec((SG, KP, NLATD * ROWS), lambda g: (g, 0, 0)),
            pl.BlockSpec((512, 1024), lambda g: (0, 0)),
            pl.BlockSpec((NPADDED // NSG, L), lambda g: (g, 0)),
            pl.BlockSpec((NPADDED // NSG, L), lambda g: (g, 0)),
            pl.BlockSpec((L, NLATD * 24), lambda g: (0, 0)),
        ],
        out_specs=[
            pl.BlockSpec((32 * MROWS, 128), lambda g: (0, 0)),
            pl.BlockSpec((SG, 2, NLATD * ROWS, ENTRIES), lambda g: (g, 0, 0, 0)),
            pl.BlockSpec((NPADDED // NSG, NLATD * 24), lambda g: (g, 0)),
            pl.BlockSpec((NPADDED // NSG, NLATD * 24), lambda g: (g, 0)),
        ],
        scratch_shapes=[
            pltpu.VMEM((NLATD, 2 * SLOTS, 2 * ROWS * CW), BF16),
            pltpu.VMEM((SLOTS, 2 * ENTRIES, NLATD * ROWS), BF16),
            pltpu.VMEM((6, NLATD * 24, 128), F32),
            pltpu.VMEM((2 * SG, NLATD * ROWS, 128), F32),
            pltpu.VMEM((32 * MROWS, 128), F32),
            pltpu.SemaphoreType.DMA((NLATD,)),
            pltpu.SemaphoreType.DMA((NLATD,)),
            pltpu.SemaphoreType.DMA,
        ],
        out_shape=[
            jax.ShapeDtypeStruct((32 * MROWS, 128), BF16),
            jax.ShapeDtypeStruct((SLOTS, 2, NLATD * ROWS, ENTRIES), BF16),
            jax.ShapeDtypeStruct((NPADDED, NLATD * 24), BF16),
            jax.ShapeDtypeStruct((NPADDED, NLATD * 24), BF16),
        ],
        compiler_params=pltpu.CompilerParams(
            vmem_limit_bytes=VMEM_LIMIT, collective_id=2, has_side_effects=True
        ),
        name="outbound_legendre",
    )(
        spectra,
        first,
        legendre,
        jnp.asarray(swap_mirror_table()),
        jnp.asarray(waves[:, :L]),
        jnp.asarray(waves[:, L:]),
        home,
    )


def opening_kernel(
    rows_ref, w_ref, left_ref, right_ref, o_ref, send_sem, recv_sem, local_sem, halo_send, halo_recv
):
    me = own_index("own")
    band = own_index("lat")
    rightward = lax.rem(band + 1, NLATD)
    leftward = lax.rem(band + NLATD - 1, NLATD)
    barrier = pltpu.get_barrier_semaphore()
    for neighbour in (leftward, rightward):
        pl.semaphore_signal(
            barrier, inc=1, device_id=partner("lat", neighbour), device_id_type=pl.DeviceIdType.MESH
        )
    greet("own", 32, barrier)
    local = pltpu.make_async_copy(w_ref.at[me], o_ref.at[me], local_sem)
    local.start()
    pl.semaphore_wait(barrier, 33)

    def halo(side, row):
        return pltpu.make_async_remote_copy(
            src_ref=rows_ref.at[side * (HALO + ROWS) + row],
            dst_ref=(left_ref if side else right_ref).at[row],
            send_sem=halo_send.at[side, row],
            recv_sem=halo_recv.at[side, row],
            device_id=partner("lat", rightward if side else leftward),
            device_id_type=pl.DeviceIdType.MESH,
        )

    def copy(k, sign):
        peer = peer_of("own", k, sign)
        return pltpu.make_async_remote_copy(
            src_ref=w_ref.at[peer],
            dst_ref=o_ref.at[me if sign == 1 else peer],
            send_sem=send_sem.at[k],
            recv_sem=recv_sem.at[k],
            device_id=partner("own", peer),
            device_id_type=pl.DeviceIdType.MESH,
        )

    for row in range(HALO):
        for side in range(2):
            halo(side, row).start()

    def start(k, carry):
        copy(k, 1).start()
        return carry

    lax.fori_loop(1, 32, start, 0)

    def finish(k, carry):
        copy(k, 1).wait_send()
        copy(k, -1).wait_recv()
        return carry

    lax.fori_loop(1, 32, finish, 0)
    local.wait()
    for side in range(2):
        for row in range(HALO):
            halo(side, row).wait_send()
            halo(side, row).wait_recv()


def run_opening(rows, by_degree):
    return pl.pallas_call(
        opening_kernel,
        in_specs=[pl.BlockSpec(memory_space=pl.ANY)] * 2,
        out_specs=[pl.BlockSpec(memory_space=pl.ANY)] * 3,
        scratch_shapes=[
            pltpu.SemaphoreType.DMA((32,)),
            pltpu.SemaphoreType.DMA((32,)),
            pltpu.SemaphoreType.DMA,
            pltpu.SemaphoreType.DMA((2, HALO)),
            pltpu.SemaphoreType.DMA((2, HALO)),
        ],
        out_shape=[
            jax.ShapeDtypeStruct((HALO, CW, NLON), BF16),
            jax.ShapeDtypeStruct((HALO, CW, NLON), BF16),
            jax.ShapeDtypeStruct(by_degree.shape, BF16),
        ],
        compiler_params=pltpu.CompilerParams(collective_id=0, has_side_effects=True),
        name="opening_exchange",
    )(rows, by_degree)


def order_columns(pairing):
    a = pairing.reshape(NLATD, 1, SLOTS)
    return jnp.where(a >= 0, jnp.concatenate([a, L - 1 - a], axis=1), -1)


def one_hot(col, width):
    return (col.reshape(-1)[:, None] == jnp.arange(width, dtype=jnp.int32)[None, :]).astype(BF16)


def dot_nt(a, b):
    return lax.dot_general(a, b, (((1,), (1,)), ((), ())), preferred_element_type=F32)


def per_device(grid_in, pairing, offsets, legendre, degree_mix, w_in, w_out):
    lat = ("y", "z")
    me = lax.axis_index("y") * NZ + lax.axis_index("z")
    chan = lax.axis_index("chan")
    start = jnp.take(offsets, me)
    length = jnp.take(offsets, me + 1) - start
    first = lax.dynamic_slice_in_dim(pairing, me * SLOTS, SLOTS)
    cap = grid_in.shape[0]

    rows = jnp.transpose(grid_in, (0, 2, 1))
    valid = (jnp.arange(cap, dtype=jnp.int32) < length)[:, None, None]
    rows = jnp.where(valid, rows, jnp.zeros((), BF16))
    shift = me * ROWS - HALO - start
    rows = jnp.concatenate([jnp.zeros((12, CW, NLON), BF16), rows], axis=0)
    virt = lax.dynamic_slice_in_dim(rows, 12 + shift, cap, axis=0)
    own = virt[HALO : HALO + ROWS]
    by_degree = dot_nt(
        jnp.asarray(degree_order()),
        jnp.transpose(degree_mix, (1, 2, 0)).reshape(8 * CW, L),
    ).astype(BF16)
    from_left, from_right, owned = run_opening(virt, by_degree.reshape(32, 2 * JO, 256))
    xt = (own + jnp.concatenate([from_left, from_right], axis=0)).reshape(ROWS * CW, NLON)
    gathered = lax.all_gather(owned, "z", axis=0, tiled=False)
    weights = run_weights(gathered)
    weights = weights.reshape(2 * JO, 256, 256)

    sides = order_columns(pairing)
    home = sides.reshape(NLATD, 2, NSG, SG).transpose(2, 0, 1, 3).reshape(-1)
    home = (jnp.arange(L, dtype=jnp.int32)[:, None] == home[None, :]).astype(BF16)
    padded = dot_nt(jnp.asarray(pad_rows()), xt).astype(BF16)

    waves = forward_table()
    by_order = lax.optimization_barrier(
        jnp.concatenate(
            [dot_nt(jnp.asarray(waves[:L]), xt).astype(BF16), dot_nt(jnp.asarray(waves[L:]), xt).astype(BF16)],
            axis=1,
        )
    )
    spectra = jnp.dot(one_hot(sides, L), by_order, preferred_element_type=F32).astype(BF16)
    coeffs, turned, inverse_re, inverse_im = run_outbound(
        spectra.reshape(NLATD, 24, 2 * ROWS * CW), first, legendre, home
    )
    at_owner = lax.all_to_all(
        coeffs.reshape(32, MROWS, 128), ("y", "chan"), split_axis=0, concat_axis=0, tiled=True
    )
    at_owner, weights, padded = lax.optimization_barrier((at_owner, weights, padded))
    owner = (lax.axis_index("y") * NCH + chan).reshape(1)
    z = lax.axis_index("z")
    a_here = lax.dynamic_slice_in_dim(pairing.reshape(NY, NZ, SLOTS), z, 1, axis=1)[:, 0]
    a_here = jnp.concatenate([a_here, jnp.full((NY, 4), -1, jnp.int32)], axis=1).reshape(1, NY * 16)
    a_here = jnp.broadcast_to(a_here, (2, NY * 16)).reshape(128, 1)
    mixed = run_mix(owner, at_owner, weights, a_here)
    spectrum, homeward = run_inverse(first, mixed.reshape(32 * MROWS, 128), turned)
    spectrum = jnp.transpose(spectrum.reshape(SLOTS, 2, CW, KP), (0, 3, 1, 2))
    homeward = homeward.reshape(NLATD * 24, 2 * ROWS * CW)
    filtered = jnp.dot(
        inverse_re, homeward[:, : ROWS * CW], preferred_element_type=F32
    ) + jnp.dot(inverse_im, homeward[:, ROWS * CW :], preferred_element_type=F32)
    state = (padded.astype(F32) + filtered).astype(BF16)
    own_rows, out_left, out_right = run_tail(state.reshape(NCH, CHUNKP, ROWS * CW), w_in, w_out)
    place = jnp.stack([shift, length])
    grid_out = run_assemble(place, (out_left, own_rows, out_right))
    grid_out = jnp.transpose(grid_out.reshape(CHUNK, cap, 256), (1, 0, 2))
    return (grid_out, spectrum)


def solution(mesh):
    fine = Mesh(np.asarray(mesh.devices).reshape(NY, NZ, NCH), ("y", "z", "chan"))
    lat = ("y", "z")
    in_specs = (
        P(lat, None, "chan"),
        P(),
        P(),
        P(lat, None, None),
        P(None, lat, "chan"),
        P(),
        P(),
    )
    out_specs = (P(lat, "chan", None), P(lat, None, None, "chan"))
    return jax.shard_map(per_device, mesh=fine, in_specs=in_specs, out_specs=out_specs, check_vma=False)
```

```python
import functools
import math

import jax
import jax.numpy as jnp
import ml_dtypes
import numpy as np
from jax import lax
from jax.experimental import pallas as pl
from jax.experimental.pallas import tpu as pltpu
from jax.sharding import Mesh
from jax.sharding import PartitionSpec as P

NLON = 1440
L = 720
KP = 721
SLOTS = 12
ROWS = 12
HALO = 6
CW = 32
NCH = 8
NY = 4
NZ = 8
NLATD = 32
CHUNK = 180
CHUNKP = 192
NPADDED = NCH * CHUNKP
JO = 12
JR = JO + 1
ENTRIES = 32 * JR
MROWS = 160
SG = 4
NSG = SLOTS // SG
EROWS = 2 * SG
F32 = jnp.float32
BF16 = jnp.bfloat16
VMEM_LIMIT = 56 * 1024 * 1024


def forward_table():
    n = np.arange(NLON, dtype=np.int64)
    m = np.arange(L, dtype=np.int64)
    ph = ((m[:, None] * n[None, :]) % NLON).astype(np.float32) * np.float32(2.0 * math.pi / NLON)
    f = np.float32(1.0 / math.sqrt(NLON))
    table = np.concatenate([np.cos(ph) * f, -np.sin(ph) * f], axis=0)
    return table.astype(ml_dtypes.bfloat16)


def inverse_table():
    n = np.arange(NLON, dtype=np.int64)
    m = np.arange(L, dtype=np.int64)
    ph = ((n[:, None] * m[None, :]) % NLON).astype(np.float32) * np.float32(2.0 * math.pi / NLON)
    f = np.float32(1.0 / math.sqrt(NLON))
    w = np.where(m == 0, 1.0, 2.0).astype(np.float32)[None, :] * f
    table = np.concatenate([np.cos(ph) * w, -np.sin(ph) * w], axis=1)
    padded = np.zeros((NCH, CHUNKP, 2 * L), np.float32)
    padded[:, :CHUNK] = table.reshape(NCH, CHUNK, 2 * L)
    return padded.reshape(NPADDED, 2 * L).astype(ml_dtypes.bfloat16)


def pad_rows():
    sel = np.zeros((NCH, CHUNKP, NLON), np.float32)
    for c in range(NCH):
        for i in range(CHUNK):
            sel[c, i, c * CHUNK + i] = 1.0
    return sel.reshape(NPADDED, NLON).astype(ml_dtypes.bfloat16)


def degree_order():
    sel = np.zeros((32, 2 * JO, L), np.float32)
    for o in range(L // 2 // JO):
        for jj in range(JO):
            j = o * JO + jj
            sel[o, jj, j] = 1.0
            sel[o, JO + jj, L - 1 - j] = 1.0
    return sel.reshape(32 * 2 * JO, L).astype(ml_dtypes.bfloat16)


def swap_table():
    sel = np.zeros((4, 4, CW, 4, 4, CW), np.float32)
    for q in range(4):
        for r in range(4):
            for c in range(CW):
                sel[q, r, c, r, q, c] = 1.0
    return sel.reshape(512, 512).astype(ml_dtypes.bfloat16)


def swap_mirror_table():
    base = swap_table().reshape(512, 4, 4, CW)
    return np.concatenate([base, base[:, :, [2, 3, 0, 1]]], axis=2).reshape(512, 1024)


def swap4(v, table):
    joined = jnp.concatenate([x.astype(BF16) for x in v], axis=1)
    out = jnp.dot(joined, table, preferred_element_type=F32)
    width = out.shape[1] // 4
    return [out[:, k * width : (k + 1) * width] for k in range(4)]


def pair_one_hots(base):
    ri = lax.broadcasted_iota(jnp.int32, (32 * JR, 1), 0)
    jj = ri // 32
    o = ri % 32
    j = JO * o + jj
    regular = (jj < JO) & (j < L // 2)
    extra = (jj == JO) & (base // JO == o)
    kx = jnp.where(regular, L - 1 - base - j, jnp.where(extra, L - base, -1))
    ky = jnp.where(regular, jnp.where(j >= base, j - base, L - j), -1)
    col = lax.broadcasted_iota(jnp.int32, (32 * JR, KP), 1)
    sx = jnp.where(col == kx, 1.0, 0.0).astype(BF16)
    sy = jnp.where(col == ky, 1.0, 0.0).astype(BF16)
    return sx, sy


def legendre_slot(s, part, base, scr_f, table, swap, scr_r, scr_o):
    row = lax.broadcasted_iota(jnp.int32, (ENTRIES, 128), 0)
    lane = lax.broadcasted_iota(jnp.int32, (ENTRIES, 128), 1)
    degree = JO * (row % 32) + row // 32
    t = [
        jnp.concatenate(
            [scr_f.at[p * 3 + rg][pl.ds(side * SLOTS + s, 32, stride=24), :] for rg in range(3)], axis=0
        )
        for side in range(2)
        for p in range(2)
    ]
    for r4, u in enumerate(swap4(t, swap)):
        for rg in range(3):
            for k in range(2):
                scr_r.at[part * 2 + k][pl.ds(rg * 4 + r4, 32, stride=ROWS), :] = u[
                    rg * 32 : rg * 32 + 32, k * 128 : k * 128 + 128
                ]
    right = jnp.concatenate([scr_r[part * 2], scr_r[part * 2 + 1]], axis=1).astype(BF16)
    both = jnp.dot(table[s], right, preferred_element_type=F32)
    x = jnp.where(row < 32 * JO, both[:ENTRIES, :128], both[:ENTRIES, 128:])
    y = jnp.where(degree >= base, both[ENTRIES:, 128:], both[ENTRIES:, :128])
    q = jnp.where(lane < 64, x, y)
    for jj in range(JR):
        scr_o[pl.ds(s * JR + jj, 32, stride=MROWS), :] = q[jj * 32 : jj * 32 + 32]


def weights_kernel(w_ref, swap_ref, out_ref, scr):
    for zz in range(2):
        unpack_one(w_ref, swap_ref, out_ref, scr, zz)


def unpack_one(w_ref, swap_ref, out_ref, scr, zz):
    for h in range(2):
        for ih in range(2):
            t = [
                jnp.concatenate(
                    [
                        w_ref[zz, y * 8 + h * 4 + c, :, ih * 128 : ih * 128 + 128].astype(F32)
                        for y in range(NY)
                    ],
                    axis=0,
                )
                for c in range(4)
            ]
            for i4, u in enumerate(swap4(t, swap_ref[...])):
                for y in range(NY):
                    scr.at[zz * 2 + h][pl.ds(y * 8 + ih * 4 + i4, 2 * JO, stride=32), :] = u[
                        y * 2 * JO : (y + 1) * 2 * JO
                    ]
    for h in range(2):
        out_ref[:, :, zz, :, h * 128 : h * 128 + 128] = scr[zz * 2 + h].astype(BF16).reshape(2 * JO, NY, 8, 128)


def run_weights(gathered):
    return pl.pallas_call(
        weights_kernel,
        grid=(NZ // 2,),
        in_specs=[
            pl.BlockSpec((2, 32, 2 * JO, 256), lambda z: (z, 0, 0, 0)),
            pl.BlockSpec((512, 512), lambda z: (0, 0)),
        ],
        out_specs=pl.BlockSpec((2 * JO, NY, 2, 8, 256), lambda z: (0, 0, z, 0, 0)),
        scratch_shapes=[pltpu.VMEM((4, 2 * JO * 32, 128), F32)],
        out_shape=jax.ShapeDtypeStruct((2 * JO, NY, NZ, 8, 256), BF16),
        cost_estimate=pl.CostEstimate(flops=4 * 10**9, bytes_accessed=6 * 10**6, transcendentals=0),
        compiler_params=pltpu.CompilerParams(vmem_limit_bytes=VMEM_LIMIT),
        name="unpack_weights",
    )(gathered, jnp.asarray(swap_table()))


VROWS = NY * MROWS


def mix_kernel(
    owner_ref, d_ref, w_ref, a_ref, swap_ref, home_ref, v, ex, leaving, send_sem, recv_sem, local_sem
):
    me = own_index("own")
    barrier = pltpu.get_barrier_semaphore()
    greet("own", 32, barrier)
    for y in range(NY):
        for h in range(2):
            t = [d_ref[y * 8 + h * 4 + i] for i in range(4)]
            for q, u in enumerate(swap4(t, swap_ref[...])):
                v[h, q * VROWS + y * MROWS : q * VROWS + (y + 1) * MROWS, :] = u
    v[:, 4 * VROWS :, :] = jnp.zeros((2, v.shape[1] - 4 * VROWS, 128), F32)
    lane_a = a_ref[...]

    def rows(q, jj):
        return jnp.concatenate(
            [
                jnp.concatenate(
                    [v.at[h][pl.ds(start, 16, stride=JR), :] for h in range(2)], axis=1
                )
                for start in (q * VROWS + y * MROWS + jj for y in range(NY))
            ],
            axis=0,
        )

    extra = jnp.concatenate([rows(0, JO), rows(1, JO)], axis=0).astype(BF16)
    ex[...] = jnp.zeros_like(ex)
    owner = owner_ref[0]

    def put(q, jj, value):
        for y in range(NY):
            start = q * VROWS + y * MROWS + jj
            for h in range(2):
                v.at[h][pl.ds(start, SLOTS, stride=JR), :] = value[
                    y * 16 : y * 16 + SLOTS, h * 128 : h * 128 + 128
                ]

    for jj in range(JO):
        j = owner * JO + jj
        x = jnp.concatenate([rows(0, jj), rows(1, jj)], axis=0).astype(BF16)
        yv = jnp.concatenate([rows(2, jj), rows(3, jj)], axis=0).astype(BF16)
        upper = jnp.dot(
            jnp.concatenate([x, yv, extra], axis=0), w_ref[JO + jj], preferred_element_type=F32
        )
        lower = jnp.dot(yv, w_ref[jj], preferred_element_type=F32)
        ym = jnp.where(lane_a <= j, lower, upper[128:256])
        ex[...] += jnp.where(lane_a == j, upper[256:384], 0.0)
        put(0, jj, upper[0:64])
        put(1, jj, upper[64:128])
        put(2, jj, ym[0:64])
        put(3, jj, ym[64:128])
    put(0, JO, ex[0:64, :])
    put(1, JO, ex[64:128, :])
    for y in range(NY):
        for h in range(2):
            t = [
                v[h, q * VROWS + y * MROWS : q * VROWS + (y + 1) * MROWS, :]
                for q in range(4)
            ]
            for i, u in enumerate(swap4(t, swap_ref[...])):
                leaving[y * 8 + h * 4 + i] = u.astype(BF16)
    local = pltpu.make_async_copy(leaving.at[me], home_ref.at[me], local_sem)
    local.start()
    pl.semaphore_wait(barrier, 31)

    def copy(k, sign):
        peer = peer_of("own", k, sign)
        return pltpu.make_async_remote_copy(
            src_ref=leaving.at[peer],
            dst_ref=home_ref.at[me if sign == 1 else peer],
            send_sem=send_sem.at[k],
            recv_sem=recv_sem.at[k],
            device_id=partner("own", peer),
            device_id_type=pl.DeviceIdType.MESH,
        )

    def start(k, carry):
        copy(k, 1).start()
        return carry

    lax.fori_loop(1, 32, start, 0)

    def finish(k, carry):
        copy(k, 1).wait_send()
        copy(k, -1).wait_recv()
        return carry

    lax.fori_loop(1, 32, finish, 0)
    local.wait()


def run_mix(owner, coeffs, weights, lower_orders):
    return pl.pallas_call(
        mix_kernel,
        in_specs=[
            pl.BlockSpec(memory_space=pltpu.SMEM),
            pl.BlockSpec(memory_space=pltpu.VMEM),
            pl.BlockSpec(memory_space=pltpu.VMEM),
            pl.BlockSpec(memory_space=pltpu.VMEM),
            pl.BlockSpec(memory_space=pltpu.VMEM),
        ],
        out_specs=pl.BlockSpec(memory_space=pl.ANY),
        scratch_shapes=[pltpu.VMEM((2, 4 * VROWS + 64, 128), F32), pltpu.VMEM((128, 256), F32),
            pltpu.VMEM((32, MROWS, 128), BF16),
            pltpu.SemaphoreType.DMA((32,)),
            pltpu.SemaphoreType.DMA((32,)),
            pltpu.SemaphoreType.DMA,
        ],
        out_shape=jax.ShapeDtypeStruct((32, MROWS, 128), BF16),
        compiler_params=pltpu.CompilerParams(
            vmem_limit_bytes=VMEM_LIMIT, collective_id=1, has_side_effects=True
        ),
        name="mix_degrees",
    )(owner, coeffs, weights, lower_orders, jnp.asarray(swap_table()))


def inverse_kernel(
    first_ref, d_ref, turned_ref, swap_ref, spec_ref, home_ref,
    scr_f, scr_b, scr_e, entries, leaving, send_sem, recv_sem, local_sem,
):
    group = pl.program_id(0)
    me = own_index("lat")
    barrier = pltpu.get_barrier_semaphore()

    @pl.when(group == 0)
    def _():
        greet("lat", NLATD, barrier)
        scr_f[...] = d_ref[...].astype(F32)

    row = lax.broadcasted_iota(jnp.int32, (ENTRIES, 128), 0)
    left = lax.broadcasted_iota(jnp.int32, (ENTRIES, 128), 1) < 64
    degree = JO * (row % 32) + row // 32
    for ss in range(SG):
        s = group * SG + ss
        q = jnp.concatenate(
            [scr_f[pl.ds(s * JR + jj, 32, stride=MROWS), :] for jj in range(JR)], axis=0
        )
        entries[s] = q.astype(BF16)
        qs = pltpu.roll(q, 64, 1)
        base = jnp.maximum(first_ref[s], 0)
        x = jnp.where(row < 32 * JO, jnp.where(left, q, 0.0), jnp.where(left, 0.0, qs)).astype(BF16)
        y = jnp.where(degree >= base, jnp.where(left, qs, 0.0), jnp.where(left, 0.0, q)).astype(BF16)
        scr_b[ss] = jnp.dot(turned_ref[ss, 0], x, preferred_element_type=F32) + jnp.dot(
            turned_ref[ss, 1], y, preferred_element_type=F32
        )
        t = [
            jnp.concatenate(
                [scr_b.at[ss][pl.ds(rg * 4 + r4, 32, stride=ROWS), :] for rg in range(3)], axis=0
            )
            for r4 in range(4)
        ]
        for qi, u in enumerate(swap4(t, swap_ref[...])):
            for rg in range(3):
                scr_e.at[(qi % 2) * 3 + rg][pl.ds((qi // 2) * SG + ss, 32, stride=EROWS), :] = u[
                    rg * 32 : rg * 32 + 32
                ]
    for k in range(6):
        leaving[group, :, :, k * 128 : k * 128 + 128] = (
            scr_e[k].reshape(NLATD, EROWS, 128).astype(BF16)
        )

    @pl.when(group == 0)
    def _():
        pl.semaphore_wait(barrier, NLATD - 1)

    def send(g, k):
        peer = peer_of("lat", k, 1)
        return pltpu.make_async_remote_copy(
            src_ref=leaving.at[g, peer],
            dst_ref=home_ref.at[g, me],
            send_sem=send_sem.at[g, k],
            recv_sem=recv_sem.at[g, k],
            device_id=partner("lat", peer),
            device_id_type=pl.DeviceIdType.MESH,
        )

    def start(k, carry):
        send(group, k).start()
        return carry

    lax.fori_loop(1, NLATD, start, 0)
    pltpu.make_async_copy(leaving.at[group, me], home_ref.at[group, me], local_sem.at[group]).start()

    @pl.when(group == NSG - 1)
    def _():
        def pack(s, carry):
            sx, sy = pair_one_hots(jnp.maximum(first_ref[s], 0))
            qt = jnp.transpose(entries[s].astype(F32)).astype(BF16)
            spec_ref[s] = (
                jnp.dot(qt[:64], sx, preferred_element_type=F32)
                + jnp.dot(qt[64:], sy, preferred_element_type=F32)
            ).astype(BF16)
            return carry

        lax.fori_loop(0, SLOTS, pack, 0)
        for g in range(NSG):

            def finish(k, carry):
                send(g, k).wait_send()
                source = peer_of("lat", k, -1)
                pltpu.make_async_remote_copy(
                    src_ref=leaving.at[g, source],
                    dst_ref=home_ref.at[g, source],
                    send_sem=send_sem.at[g, k],
                    recv_sem=recv_sem.at[g, k],
                    device_id=partner("lat", source),
                    device_id_type=pl.DeviceIdType.MESH,
                ).wait_recv()
                return carry

            lax.fori_loop(1, NLATD, finish, 0)
            pltpu.make_async_copy(leaving.at[g, me], home_ref.at[g, me], local_sem.at[g]).wait()


def run_inverse(first, mixed, turned):
    return pl.pallas_call(
        inverse_kernel,
        grid=(NSG,),
        in_specs=[
            pl.BlockSpec(memory_space=pltpu.SMEM),
            pl.BlockSpec((32 * MROWS, 128), lambda g: (0, 0)),
            pl.BlockSpec((SG, 2, NLATD * ROWS, ENTRIES), lambda g: (g, 0, 0, 0)),
            pl.BlockSpec((512, 512), lambda g: (0, 0)),
        ],
        out_specs=[
            pl.BlockSpec((SLOTS, 2 * CW, KP), lambda g: (0, 0, 0)),
            pl.BlockSpec(memory_space=pl.ANY),
        ],
        scratch_shapes=[
            pltpu.VMEM((32 * MROWS, 128), F32),
            pltpu.VMEM((SG, NLATD * ROWS, 128), F32),
            pltpu.VMEM((6, NLATD * EROWS, 128), F32),
            pltpu.VMEM((SLOTS, ENTRIES, 128), BF16),
            pltpu.VMEM((NSG, NLATD, EROWS, 2 * ROWS * CW), BF16),
            pltpu.SemaphoreType.DMA((NSG, NLATD)),
            pltpu.SemaphoreType.DMA((NSG, NLATD)),
            pltpu.SemaphoreType.DMA((NSG,)),
        ],
        out_shape=[
            jax.ShapeDtypeStruct((SLOTS, 2 * CW, KP), BF16),
            jax.ShapeDtypeStruct((NSG, NLATD, EROWS, 2 * ROWS * CW), BF16),
        ],
        compiler_params=pltpu.CompilerParams(
            vmem_limit_bytes=VMEM_LIMIT, collective_id=3, has_side_effects=True
        ),
        name="legendre_inverse_home",
    )(first, mixed, turned, jnp.asarray(swap_table()))


GROUP_ORDER = (0, 2, 1)
PIECES = ((0, 4, 0), (4, 6, 4), (6, 8, 0), (8, 12, 2))


def tail_kernel(
    x_ref, w_in_ref, w_out_ref, swap_ref, own_ref, left_ref, right_ref,
    recv, res, v, send_sem, recv_sem, local_sem, halo_send, halo_recv, own_sem,
):
    me = own_index("chan")
    band = own_index("lat")
    rightward = lax.rem(band + 1, NLATD)
    leftward = lax.rem(band + NLATD - 1, NLATD)
    barrier = pltpu.get_barrier_semaphore()
    greet("chan", NCH, barrier)
    for neighbour in (leftward, rightward):
        pl.semaphore_signal(
            barrier, inc=1, device_id=partner("lat", neighbour), device_id_type=pl.DeviceIdType.MESH
        )

    def local(rg):
        at = pl.ds(rg * 128, 128)
        return pltpu.make_async_copy(x_ref.at[me, :, at], recv.at[me, :, at], local_sem.at[rg])

    for rg in range(3):
        local(rg).start()
    pl.semaphore_wait(barrier, NCH + 1)

    def copy(rg, k, sign):
        peer = peer_of("chan", k, sign)
        at = pl.ds(rg * 128, 128)
        return pltpu.make_async_remote_copy(
            src_ref=x_ref.at[peer, :, at],
            dst_ref=recv.at[me if sign == 1 else peer, :, at],
            send_sem=send_sem.at[rg, k],
            recv_sem=recv_sem.at[rg, k],
            device_id=partner("chan", peer),
            device_id_type=pl.DeviceIdType.MESH,
        )

    def start_group(rg):
        def start(k, carry):
            copy(rg, k, 1).start()
            return carry

        lax.fori_loop(1, NCH, start, 0)

    def group_left(rg):
        def finish(k, carry):
            copy(rg, k, 1).wait_send()
            return carry

        lax.fori_loop(1, NCH, finish, 0)

    start_group(GROUP_ORDER[0])

    def halo(piece):
        first, last, place = PIECES[piece]
        there = right_ref if piece < 2 else left_ref
        return pltpu.make_async_remote_copy(
            src_ref=res.at[pl.ds(first, last - first)],
            dst_ref=there.at[pl.ds(place, last - first)],
            send_sem=halo_send.at[piece],
            recv_sem=halo_recv.at[piece],
            device_id=partner("lat", leftward if piece < 2 else rightward),
            device_id_type=pl.DeviceIdType.MESH,
        )

    for place, rg in enumerate(GROUP_ORDER):
        group_left(rg)
        if place < 2:
            start_group(GROUP_ORDER[place + 1])

        def arrive(k, carry):
            copy(rg, k, -1).wait_recv()
            return carry

        lax.fori_loop(1, NCH, arrive, 0)
        local(rg).wait()
        for h in range(2):
            t = [recv[h * 4 + i, :, rg * 128 : rg * 128 + 128] for i in range(4)]
            for r4, u in enumerate(swap4(t, swap_ref[...])):
                v[r4 * CHUNKP : (r4 + 1) * CHUNKP, h * 128 : h * 128 + 128] = u
        values = v[...]
        centered = values - jnp.mean(values, axis=-1, keepdims=True)
        normed = (
            centered * lax.rsqrt(jnp.mean(centered * centered, axis=-1, keepdims=True) + 1e-05)
        ).astype(BF16)
        hidden = jax.nn.gelu(
            jnp.dot(normed, w_in_ref[...], preferred_element_type=F32), approximate=True
        ).astype(BF16)
        result = (values + jnp.dot(hidden, w_out_ref[...], preferred_element_type=F32)).astype(BF16)
        for r4 in range(4):
            res[rg * 4 + r4] = result[r4 * CHUNKP : r4 * CHUNKP + CHUNK]
        for piece in ((0,), (1, 2), (3,))[rg]:
            halo(piece).start()
    own = pltpu.make_async_copy(res, own_ref, own_sem)
    own.start()
    for piece in range(4):
        halo(piece).wait_send()
        halo(piece).wait_recv()
    own.wait()


def run_tail(state, w_in, w_out):
    return pl.pallas_call(
        tail_kernel,
        in_specs=[pl.BlockSpec(memory_space=pl.ANY)] + [pl.BlockSpec(memory_space=pltpu.VMEM)] * 3,
        out_specs=[pl.BlockSpec(memory_space=pl.ANY)] * 3,
        scratch_shapes=[
            pltpu.VMEM((NCH, CHUNKP, ROWS * CW), BF16),
            pltpu.VMEM((ROWS, CHUNK, 256), BF16),
            pltpu.VMEM((4 * CHUNKP, 256), F32),
            pltpu.SemaphoreType.DMA((3, NCH)),
            pltpu.SemaphoreType.DMA((3, NCH)),
            pltpu.SemaphoreType.DMA((3,)),
            pltpu.SemaphoreType.DMA((4,)),
            pltpu.SemaphoreType.DMA((4,)),
            pltpu.SemaphoreType.DMA,
        ],
        out_shape=[
            jax.ShapeDtypeStruct((ROWS, CHUNK, 256), BF16),
            jax.ShapeDtypeStruct((HALO, CHUNK, 256), BF16),
            jax.ShapeDtypeStruct((HALO, CHUNK, 256), BF16),
        ],
        compiler_params=pltpu.CompilerParams(
            vmem_limit_bytes=VMEM_LIMIT, collective_id=4, has_side_effects=True
        ),
        name="pointwise_tail",
    )(state, w_in, w_out, jnp.asarray(swap_table()))


def assemble_kernel(place_ref, left_ref, own_ref, right_ref, out_ref, scr):
    scr[...] = jnp.zeros_like(scr)
    for at, ref in ((0, left_ref), (HALO, own_ref), (HALO + ROWS, right_ref)):
        for k in range(ref.shape[0]):
            row = at + k + place_ref[0]

            @pl.when((row >= 0) & (row < place_ref[1]))
            def _():
                for h in range(2):
                    scr.at[h][pl.ds(row, CHUNK, stride=24), :] = ref[
                        k, :, h * 128 : h * 128 + 128
                    ].astype(F32)

    for h in range(2):
        out_ref[:, h * 128 : h * 128 + 128] = scr[h].astype(BF16)


def run_assemble(place, pieces):
    return pl.pallas_call(
        assemble_kernel,
        in_specs=[pl.BlockSpec(memory_space=pltpu.SMEM)] + [pl.BlockSpec(memory_space=pltpu.VMEM)] * 3,
        out_specs=pl.BlockSpec(memory_space=pltpu.VMEM),
        scratch_shapes=[pltpu.VMEM((2, CHUNK * 24, 128), F32)],
        out_shape=jax.ShapeDtypeStruct((CHUNK * 24, 256), BF16),
        compiler_params=pltpu.CompilerParams(vmem_limit_bytes=VMEM_LIMIT),
        name="assemble_bands",
    )(place, *pieces)


def partner(kind, index):
    y, z, c = lax.axis_index("y"), lax.axis_index("z"), lax.axis_index("chan")
    if kind == "lat":
        return (index // NZ, index % NZ, c)
    if kind == "own":
        return (index // NCH, z, index % NCH)
    return (y, z, index)


def own_index(kind):
    y, z, c = lax.axis_index("y"), lax.axis_index("z"), lax.axis_index("chan")
    if kind == "lat":
        return y * NZ + z
    if kind == "own":
        return y * NCH + c
    return c


def zigzag(j, n):
    half = (j + 1) // 2
    return jnp.where(j % 2 == 1, half, lax.rem(n - half, n))


def peer_of(kind, k, sign):
    me = own_index(kind)
    if kind == "chan":
        return lax.rem(me + sign * k + NCH, NCH)
    n = NLATD - k
    fast, slow = n // NY, n % NY
    y = lax.rem(me // 8 + sign * zigzag(slow, NY) + NY, NY)
    low = me % 8
    if kind == "lat":
        return y * 8 + lax.rem(low + sign * zigzag(fast, NZ) + NZ, NZ)
    x = lax.rem(low // 2 + sign * zigzag(fast // 2, 4) + 4, 4)
    return y * 8 + x * 2 + lax.rem(low % 2 + fast % 2, 2)


def greet(kind, n, barrier):
    me = own_index(kind)

    def one(k, carry):
        pl.semaphore_signal(
            barrier,
            inc=1,
            device_id=partner(kind, lax.rem(me + k, n)),
            device_id_type=pl.DeviceIdType.MESH,
        )
        return carry

    lax.fori_loop(1, n, one, 0)


def outbound_kernel(
    x_ref, first_ref, leg_ref, swap_ref, wave_re_ref, wave_im_ref, home_ref,
    coeff_ref, turned_ref, inverse_re_ref, inverse_im_ref,
    arrived, table, scr_f, scr_r, scr_o, send_sem, recv_sem, local_sem,
):
    group = pl.program_id(0)
    me = own_index("lat")
    barrier = pltpu.get_barrier_semaphore()
    local = pltpu.make_async_copy(x_ref.at[me], arrived.at[me], local_sem)

    def copy(k, sign):
        peer = peer_of("lat", k, sign)
        return pltpu.make_async_remote_copy(
            src_ref=x_ref.at[peer],
            dst_ref=arrived.at[me if sign == 1 else peer],
            send_sem=send_sem.at[k],
            recv_sem=recv_sem.at[k],
            device_id=partner("lat", peer),
            device_id_type=pl.DeviceIdType.MESH,
        )

    @pl.when(group == 0)
    def _():
        greet("lat", NLATD, barrier)
        local.start()
        pl.semaphore_wait(barrier, NLATD - 1)

        def start(k, carry):
            copy(k, 1).start()
            return carry

        lax.fori_loop(1, NLATD, start, 0)

    for ss in range(SG):
        sx, sy = pair_one_hots(jnp.maximum(first_ref[group * SG + ss], 0))
        packed = leg_ref[ss]
        x = jnp.dot(sx, packed, preferred_element_type=F32)
        y = jnp.dot(sy, packed, preferred_element_type=F32)
        table[group * SG + ss, :ENTRIES] = x.astype(BF16)
        table[group * SG + ss, ENTRIES:] = y.astype(BF16)
        turned_ref[ss, 0] = jnp.transpose(x).astype(BF16)
        turned_ref[ss, 1] = jnp.transpose(y).astype(BF16)
    inverse_re_ref[...] = jnp.dot(
        wave_re_ref[...], home_ref[...], preferred_element_type=F32
    ).astype(BF16)
    inverse_im_ref[...] = jnp.dot(
        wave_im_ref[...], home_ref[...], preferred_element_type=F32
    ).astype(BF16)

    @pl.when(group == NSG - 1)
    def _():
        def finish(k, carry):
            copy(k, 1).wait_send()
            copy(k, -1).wait_recv()
            return carry

        lax.fori_loop(1, NLATD, finish, 0)
        local.wait()
        for k in range(6):
            scr_f[k] = (
                arrived[:, :, k * 128 : k * 128 + 128].astype(F32).reshape(NLATD * 2 * SLOTS, 128)
            )
        scr_o[...] = jnp.zeros_like(scr_o)

        def four(g, carry):
            for ss in range(SG):
                s = g * SG + ss
                base = jnp.maximum(first_ref[s], 0)
                legendre_slot(s, ss, base, scr_f, table, swap_ref[...], scr_r, scr_o)
            return carry

        lax.fori_loop(0, NSG, four, 0)
        coeff_ref[...] = scr_o[...].astype(BF16)


def run_outbound(spectra, first, legendre, home):
    waves = inverse_table()
    return pl.pallas_call(
        outbound_kernel,
        grid=(NSG,),
        in_specs=[
            pl.BlockSpec(memory_space=pl.ANY),
            pl.BlockSpec(memory_space=pltpu.SMEM),
            pl.BlockSpec((SG, KP, NLATD * ROWS), lambda g: (g, 0, 0)),
            pl.BlockSpec((512, 1024), lambda g: (0, 0)),
            pl.BlockSpec((NPADDED // NSG, L), lambda g: (g, 0)),
            pl.BlockSpec((NPADDED // NSG, L), lambda g: (g, 0)),
            pl.BlockSpec((L, NLATD * 24), lambda g: (0, 0)),
        ],
        out_specs=[
            pl.BlockSpec((32 * MROWS, 128), lambda g: (0, 0)),
            pl.BlockSpec((SG, 2, NLATD * ROWS, ENTRIES), lambda g: (g, 0, 0, 0)),
            pl.BlockSpec((NPADDED // NSG, NLATD * 24), lambda g: (g, 0)),
            pl.BlockSpec((NPADDED // NSG, NLATD * 24), lambda g: (g, 0)),
        ],
        scratch_shapes=[
            pltpu.VMEM((NLATD, 2 * SLOTS, 2 * ROWS * CW), BF16),
            pltpu.VMEM((SLOTS, 2 * ENTRIES, NLATD * ROWS), BF16),
            pltpu.VMEM((6, NLATD * 24, 128), F32),
            pltpu.VMEM((2 * SG, NLATD * ROWS, 128), F32),
            pltpu.VMEM((32 * MROWS, 128), F32),
            pltpu.SemaphoreType.DMA((NLATD,)),
            pltpu.SemaphoreType.DMA((NLATD,)),
            pltpu.SemaphoreType.DMA,
        ],
        out_shape=[
            jax.ShapeDtypeStruct((32 * MROWS, 128), BF16),
            jax.ShapeDtypeStruct((SLOTS, 2, NLATD * ROWS, ENTRIES), BF16),
            jax.ShapeDtypeStruct((NPADDED, NLATD * 24), BF16),
            jax.ShapeDtypeStruct((NPADDED, NLATD * 24), BF16),
        ],
        compiler_params=pltpu.CompilerParams(
            vmem_limit_bytes=VMEM_LIMIT, collective_id=2, has_side_effects=True
        ),
        name="outbound_legendre",
    )(
        spectra,
        first,
        legendre,
        jnp.asarray(swap_mirror_table()),
        jnp.asarray(waves[:, :L]),
        jnp.asarray(waves[:, L:]),
        home,
    )


def opening_kernel(
    rows_ref, w_ref, left_ref, right_ref, o_ref, send_sem, recv_sem, local_sem, halo_send, halo_recv
):
    me = own_index("own")
    band = own_index("lat")
    rightward = lax.rem(band + 1, NLATD)
    leftward = lax.rem(band + NLATD - 1, NLATD)
    barrier = pltpu.get_barrier_semaphore()
    for neighbour in (leftward, rightward):
        pl.semaphore_signal(
            barrier, inc=1, device_id=partner("lat", neighbour), device_id_type=pl.DeviceIdType.MESH
        )
    greet("own", 32, barrier)
    local = pltpu.make_async_copy(w_ref.at[me], o_ref.at[me], local_sem)
    local.start()
    pl.semaphore_wait(barrier, 33)

    def halo(side, row):
        return pltpu.make_async_remote_copy(
            src_ref=rows_ref.at[side * (HALO + ROWS) + row],
            dst_ref=(left_ref if side else right_ref).at[row],
            send_sem=halo_send.at[side, row],
            recv_sem=halo_recv.at[side, row],
            device_id=partner("lat", rightward if side else leftward),
            device_id_type=pl.DeviceIdType.MESH,
        )

    def copy(k, sign):
        peer = peer_of("own", k, sign)
        return pltpu.make_async_remote_copy(
            src_ref=w_ref.at[peer],
            dst_ref=o_ref.at[me if sign == 1 else peer],
            send_sem=send_sem.at[k],
            recv_sem=recv_sem.at[k],
            device_id=partner("own", peer),
            device_id_type=pl.DeviceIdType.MESH,
        )

    for row in range(HALO):
        for side in range(2):
            halo(side, row).start()

    def start(k, carry):
        copy(k, 1).start()
        return carry

    lax.fori_loop(1, 32, start, 0)

    def finish(k, carry):
        copy(k, 1).wait_send()
        copy(k, -1).wait_recv()
        return carry

    lax.fori_loop(1, 32, finish, 0)
    local.wait()
    for side in range(2):
        for row in range(HALO):
            halo(side, row).wait_send()
            halo(side, row).wait_recv()


def run_opening(rows, by_degree):
    return pl.pallas_call(
        opening_kernel,
        in_specs=[pl.BlockSpec(memory_space=pl.ANY)] * 2,
        out_specs=[pl.BlockSpec(memory_space=pl.ANY)] * 3,
        scratch_shapes=[
            pltpu.SemaphoreType.DMA((32,)),
            pltpu.SemaphoreType.DMA((32,)),
            pltpu.SemaphoreType.DMA,
            pltpu.SemaphoreType.DMA((2, HALO)),
            pltpu.SemaphoreType.DMA((2, HALO)),
        ],
        out_shape=[
            jax.ShapeDtypeStruct((HALO, CW, NLON), BF16),
            jax.ShapeDtypeStruct((HALO, CW, NLON), BF16),
            jax.ShapeDtypeStruct(by_degree.shape, BF16),
        ],
        compiler_params=pltpu.CompilerParams(collective_id=0, has_side_effects=True),
        name="opening_exchange",
    )(rows, by_degree)


def order_columns(pairing):
    a = pairing.reshape(NLATD, 1, SLOTS)
    return jnp.where(a >= 0, jnp.concatenate([a, L - 1 - a], axis=1), -1)


def one_hot(col, width):
    return (col.reshape(-1)[:, None] == jnp.arange(width, dtype=jnp.int32)[None, :]).astype(BF16)


def dot_nt(a, b):
    return lax.dot_general(a, b, (((1,), (1,)), ((), ())), preferred_element_type=F32)


def per_device(grid_in, pairing, offsets, legendre, degree_mix, w_in, w_out):
    lat = ("y", "z")
    me = lax.axis_index("y") * NZ + lax.axis_index("z")
    chan = lax.axis_index("chan")
    start = jnp.take(offsets, me)
    length = jnp.take(offsets, me + 1) - start
    first = lax.dynamic_slice_in_dim(pairing, me * SLOTS, SLOTS)
    cap = grid_in.shape[0]

    rows = jnp.transpose(grid_in, (0, 2, 1))
    shift = me * ROWS - HALO - start
    rows = jnp.concatenate([jnp.zeros((12, CW, NLON), BF16), rows], axis=0)
    virt = lax.dynamic_slice_in_dim(rows, 12 + shift, cap, axis=0)
    stored = jnp.arange(cap, dtype=jnp.int32) + shift
    virt = jnp.where(((stored >= 0) & (stored < length))[:, None, None], virt, jnp.zeros((), BF16))
    own = virt[HALO : HALO + ROWS]
    by_degree = dot_nt(
        jnp.asarray(degree_order()),
        jnp.transpose(degree_mix, (1, 2, 0)).reshape(8 * CW, L),
    ).astype(BF16)
    from_left, from_right, owned = run_opening(virt, by_degree.reshape(32, 2 * JO, 256))
    xt = (own + jnp.concatenate([from_left, from_right], axis=0)).reshape(ROWS * CW, NLON)
    gathered = lax.all_gather(owned, "z", axis=0, tiled=False)
    weights = run_weights(gathered)
    weights = weights.reshape(2 * JO, 256, 256)

    sides = order_columns(pairing)
    home = sides.reshape(NLATD, 2, NSG, SG).transpose(2, 0, 1, 3).reshape(-1)
    home = (jnp.arange(L, dtype=jnp.int32)[:, None] == home[None, :]).astype(BF16)
    padded = dot_nt(jnp.asarray(pad_rows()), xt).astype(BF16)

    waves = forward_table()
    by_order = lax.optimization_barrier(
        jnp.concatenate(
            [dot_nt(jnp.asarray(waves[:L]), xt).astype(BF16), dot_nt(jnp.asarray(waves[L:]), xt).astype(BF16)],
            axis=1,
        )
    )
    spectra = jnp.dot(one_hot(sides, L), by_order, preferred_element_type=F32).astype(BF16)
    coeffs, turned, inverse_re, inverse_im = run_outbound(
        spectra.reshape(NLATD, 24, 2 * ROWS * CW), first, legendre, home
    )
    at_owner = lax.all_to_all(
        coeffs.reshape(32, MROWS, 128), ("y", "chan"), split_axis=0, concat_axis=0, tiled=True
    )
    at_owner, weights, padded = lax.optimization_barrier((at_owner, weights, padded))
    owner = (lax.axis_index("y") * NCH + chan).reshape(1)
    z = lax.axis_index("z")
    a_here = lax.dynamic_slice_in_dim(pairing.reshape(NY, NZ, SLOTS), z, 1, axis=1)[:, 0]
    a_here = jnp.concatenate([a_here, jnp.full((NY, 4), -1, jnp.int32)], axis=1).reshape(1, NY * 16)
    a_here = jnp.broadcast_to(a_here, (2, NY * 16)).reshape(128, 1)
    mixed = run_mix(owner, at_owner, weights, a_here)
    spectrum, homeward = run_inverse(first, mixed.reshape(32 * MROWS, 128), turned)
    spectrum = jnp.transpose(spectrum.reshape(SLOTS, 2, CW, KP), (0, 3, 1, 2))
    homeward = homeward.reshape(NLATD * 24, 2 * ROWS * CW)
    filtered = jnp.dot(
        inverse_re, homeward[:, : ROWS * CW], preferred_element_type=F32
    ) + jnp.dot(inverse_im, homeward[:, ROWS * CW :], preferred_element_type=F32)
    state = (padded.astype(F32) + filtered).astype(BF16)
    own_rows, out_left, out_right = run_tail(state.reshape(NCH, CHUNKP, ROWS * CW), w_in, w_out)
    place = jnp.stack([shift, length])
    grid_out = run_assemble(place, (out_left, own_rows, out_right))
    grid_out = jnp.transpose(grid_out.reshape(CHUNK, cap, 256), (1, 0, 2))
    return (grid_out, spectrum)


def solution(mesh):
    fine = Mesh(np.asarray(mesh.devices).reshape(NY, NZ, NCH), ("y", "z", "chan"))
    lat = ("y", "z")
    in_specs = (
        P(lat, None, "chan"),
        P(),
        P(),
        P(lat, None, None),
        P(None, lat, "chan"),
        P(),
        P(),
    )
    out_specs = (P(lat, "chan", None), P(lat, None, None, "chan"))
    return jax.shard_map(per_device, mesh=fine, in_specs=in_specs, out_specs=out_specs, check_vma=False)
```
